128 devices in a mesh: ctx: 16 (over x, z_hi, core), ch: 8 (over z_lo, y).
Axes of the slice: x: 4, y: 4, z: 4 (z_hi: 2, z_lo: 2; z = z_hi * 2 + z_lo), core: 2. Of those that a mesh axis runs over, the one named last changes fastest.
Arguments:
- tokens: bfloat16 [4096, 4096], P('ctx', 'ch'), may hold values from -6 to 6
- filter_taps: bfloat16 [4096, 4096], P('ctx', 'ch'), may hold values from -1 to 1
- block_order: int32 [32], replicated, may hold values from 0 to 31, each once
- in_weights: bfloat16 [3, 4096, 4096], P(None, None, 'ch'), may hold values from -0.09375 to 0.09375
- out_weights: bfloat16 [4096, 4096], P('ch'), may hold values from -0.09375 to 0.09375
Outputs:
- layer_out: bfloat16 [4096, 4096], P('ctx', 'ch')
The draws below stay inside these ranges and needn't reach their ends.
Inputs may be any that keep to these rules, and one draw needn't show every extreme that they name: `block_order`: each of 0 to 31 appears once.
All inputs are finite; a program needn't handle non-finite values.
Results may differ from the reference program's by a relative error of at most 0.019.
Values may be sent and summed in bfloat16 or wider, within the bound.
A program may use at most 192 MiB of HBM per device.

```python
import math
import jax
import jax.numpy as jnp
from jax import lax

D = 4096
TOKENS = 4096
BLOCKS = 32


def draw_filter_taps(key, part):
    key = jax.random.fold_in(key, 7)
    lagged = jnp.arange(TOKENS, dtype=jnp.int32)[:, None].astype(jnp.float32)
    noise = jnp.clip(jax.random.normal(key, (TOKENS, D), jnp.float32), -4.0, 4.0)
    scale = (2.0 * jnp.sqrt(jnp.float32(TOKENS))) ** (-0.5) * (lagged + 1.0) ** (-0.25)
    return (noise * scale).astype(jnp.bfloat16)


def block_levels(key, shape, cuts, least, high):
    loudness = 1.0
    for position, shards_of in cuts:
        steps = jax.random.uniform(jax.random.fold_in(jax.random.fold_in(key, 6), position), (shards_of,), jnp.float32, least / len(cuts), high / len(cuts))
        loudness = loudness * jnp.repeat(jnp.exp(steps), shape[position] // shards_of).reshape((-1,) + (1,) * (len(shape) - 1 - position))
    return loudness


def gaussian(own_key, shape, deviation, most, shards=(), kind=jnp.bfloat16):
    array = jax.random.normal(own_key, shape, jnp.float32) * deviation
    if len(shards) > 0:
        array = block_levels(own_key, shape, shards, -0.22, 0.18) * array
    return jnp.clip(array, min=-most, max=most).astype(kind)


def setup_inputs(seed: int = 0) -> dict:
    seeds = jax.random.split(jax.random.key(seed), 6)
    tokens = gaussian(seeds[0], (TOKENS, D), 1.0, 6.0, ((0, 16), (1, 8)))
    filter_taps = draw_filter_taps(jax.random.fold_in(seeds[5], 71), 0)
    block_order = jax.random.permutation(seeds[2], BLOCKS).astype(jnp.int32)
    in_weights = gaussian(seeds[3], (3, D, D), D ** -0.5, 0.09375, ((2, 8),))
    out_weights = gaussian(seeds[4], (D, D), D ** -0.5, 0.09375, ((0, 8),))
    return {"tokens": tokens, "filter_taps": filter_taps, "block_order": block_order, "in_weights": in_weights, "out_weights": out_weights}


def dft_tables(block_len):
    length = 2 * block_len
    frequency = jnp.arange(length, dtype=jnp.int32)
    angles = ((frequency[:, None] * frequency[None, :]) % length).astype(jnp.float32) * (2.0 * math.pi / length)
    forward = jnp.concatenate([jnp.cos(angles), -jnp.sin(angles)], 0).astype(jnp.bfloat16)
    later = jnp.arange(block_len, dtype=jnp.int32) + block_len
    back_angles = ((later[:, None] * frequency[None, :]) % length).astype(jnp.float32) * (2.0 * math.pi / length)
    inverse = jnp.concatenate([jnp.cos(back_angles), -jnp.sin(back_angles)], 1).astype(jnp.bfloat16)
    return forward, inverse


def reference(tokens, filter_taps, block_order, in_weights, out_weights):
    blocks = block_order.shape[0]
    block_len = tokens.shape[0] // blocks
    length = 2 * block_len
    width = tokens.shape[1]
    forward, inverse = dft_tables(block_len)
    projected = [jnp.dot(tokens, in_weights[stream], preferred_element_type=jnp.float32).astype(jnp.bfloat16) for stream in range(3)]
    mixed = (projected[0].astype(jnp.float32) * projected[2].astype(jnp.float32)).astype(jnp.bfloat16)
    stored = mixed.reshape(blocks, block_len, width)
    natural = jnp.zeros_like(stored).at[block_order].set(stored)
    block_spectra = jnp.einsum('fn,knc->kfc', forward[:, :block_len].astype(jnp.float32), natural.astype(jnp.float32)).astype(jnp.bfloat16)
    padded = jnp.concatenate([jnp.zeros((block_len, width), filter_taps.dtype), filter_taps], 0).reshape(blocks + 1, block_len, width)
    pairs = jnp.concatenate([padded[:-1], padded[1:]], 1)
    filter_spectra = jnp.einsum('fn,knc->kfc', forward.astype(jnp.float32), pairs.astype(jnp.float32)).astype(jnp.bfloat16)
    sources = jnp.arange(blocks, dtype=jnp.int32)
    data = block_spectra.astype(jnp.float32)
    data_real = data[:, :length]
    data_imag = data[:, length:]

    def one_block(target):
        lag_index = target - sources
        causal = (lag_index >= 0)[:, None, None]
        picked = jnp.take(filter_spectra, jnp.maximum(lag_index, 0), axis=0).astype(jnp.float32)
        filt_real = picked[:, :length]
        filt_imag = picked[:, length:]
        part_real = jnp.sum(jnp.where(causal, data_real * filt_real - data_imag * filt_imag, 0.0), 0)
        part_imag = jnp.sum(jnp.where(causal, data_real * filt_imag + data_imag * filt_real, 0.0), 0)
        spectrum = jnp.concatenate([part_real, part_imag], 0).astype(jnp.bfloat16)
        return jnp.dot(inverse, spectrum, preferred_element_type=jnp.float32) * (1.0 / length)

    filtered_natural = lax.map(one_block, sources)
    filtered = filtered_natural[block_order].reshape(blocks * block_len, width)
    gated = (projected[1].astype(jnp.float32) * filtered).astype(jnp.bfloat16)
    return jnp.dot(gated, out_weights, preferred_element_type=jnp.float32).astype(jnp.bfloat16)
```

```python
import functools
import math

import jax
import jax.numpy as jnp
import ml_dtypes
import numpy as np
from jax import lax
from jax.experimental import pallas as pl
from jax.experimental.pallas import tpu as pltpu
from jax.sharding import PartitionSpec as P

F32 = jnp.float32
BF16 = jnp.bfloat16


def spectral_tables(block):
    length = 2 * block
    index = np.arange(block)
    angles = 2.0 * math.pi * ((index[:, None] * index[None, :]) % length) / length
    real, imag = np.cos(angles), -np.sin(angles)
    imag[:, 0] = 1.0 - 2.0 * (index % 2)
    forward = np.concatenate([real, imag], 1).astype(ml_dtypes.bfloat16)
    later = index + block
    back = 2.0 * math.pi * ((index[:, None] * later[None, :]) % length) / length
    real, imag = 2.0 * np.cos(back) / length, -2.0 * np.sin(back) / length
    real[0] = 1.0 / length
    imag[0] = (1.0 - 2.0 * (later % 2)) / length
    inverse = np.concatenate([real, imag], 0).astype(ml_dtypes.bfloat16)
    return forward, inverse


GATHER_ORDER = (
    (0, 0), (0, 1), (1, 0), (2, 1), (3, 0), (1, 1), (2, 0), (3, 1),
    (4, 0), (4, 1), (5, 0), (6, 0), (7, 0), (5, 1), (6, 1), (7, 1),
)


def kernel(
    dims, order_ref, tokens_ref, taps_ref, w_in_ref, w_out_ref, tab_f_ref, tab_i_ref, out_ref,
    tok, wv, wo, acc, tab_f, tab_i, taps_v, taps_t, ft, fr, fi, fz, mt, mx, xn, sp, tot, yn, ys, yr,
    p1t, gated, part, rin, rout, inv_ref,
    load_sem, w_sem, wo_sem, ag_send, ag_recv, ft_send, ft_recv, mx_send, mx_recv, yr_send, yr_recv,
    rs_send, rs_recv, own_sem,
):
    nctx, nch, rows, width, block_len, block = dims
    half = width // 2
    ny = nch // 2
    chans = width // nctx
    blocks = nctx * rows // block_len
    held = rows // block_len
    long_blocks = nctx * rows // block
    per_long = block // block_len
    me = lax.axis_index("ctx")
    ch = lax.axis_index("ch")
    z = ch // ny
    y = ch % ny
    zo = 1 - z
    y_up = (y + 1) % ny
    y_dn = (y + ny - 1) % ny
    y_far = (y + 2) % ny
    up = {"ch": z * ny + y_up}
    dn = {"ch": z * ny + y_dn}
    over = {"ch": zo * ny + y}
    shard_of = (
        z * ny + y, z * ny + y_dn, z * ny + y_up, zo * ny + y,
        z * ny + y_far, zo * ny + y_dn, zo * ny + y_up, zo * ny + y_far,
    )

    def own_load(h):
        return pltpu.make_async_copy(
            tokens_ref.at[:, pl.ds(h * half, half)], tok.at[h], load_sem.at[h]
        )

    def w_load(slot, h):
        start = pl.multiple_of(shard_of[slot] * width + h * half, half)
        return pltpu.make_async_copy(
            w_in_ref.at[:, pl.ds(start, half), :], wv.at[slot * 2 + h], w_sem.at[slot * 2 + h]
        )

    def wo_load(slot, h):
        start = pl.multiple_of(shard_of[slot] * width + h * half, half)
        return pltpu.make_async_copy(
            w_out_ref.at[:, pl.ds(start, half)], wo.at[slot * 2 + h], wo_sem.at[slot * 2 + h]
        )

    taps_load = pltpu.make_async_copy(taps_ref, taps_v, load_sem.at[2])
    tab_f_load = pltpu.make_async_copy(tab_f_ref, tab_f, load_sem.at[3])
    tab_i_load = pltpu.make_async_copy(tab_i_ref, tab_i, load_sem.at[4])
    taps_load.start()
    own_load(0).start()
    own_load(1).start()

    barrier = pltpu.get_barrier_semaphore()
    for neighbour in (up, dn, over):
        pl.semaphore_signal(barrier, inc=1, device_id=neighbour, device_id_type=pl.DeviceIdType.MESH)

    def greet(d, c):
        pl.semaphore_signal(
            barrier, inc=1, device_id={"ctx": (me + d) % nctx}, device_id_type=pl.DeviceIdType.MESH
        )
        return c

    lax.fori_loop(1, nctx, greet, 0)

    for slot, h in GATHER_ORDER[:8]:
        w_load(slot, h).start()
    tab_f_load.start()
    for slot, h in GATHER_ORDER[8:]:
        w_load(slot, h).start()
    tab_i_load.start()
    for slot in (7, 6, 5, 4, 3, 2, 1, 0):
        for h in range(2):
            wo_load(slot, h).start()

    taps_load.wait()
    for r in range(0, rows, 128):
        for c in range(0, width, 128):
            piece = taps_v[r : r + 128, c : c + 128].astype(F32)
            taps_t[c : c + 128, r : r + 128] = piece.T.astype(BF16)

    pl.semaphore_wait(barrier, 3 + nctx - 1)

    def message(slot, h, source, target):
        m = (slot - 1) * 2 + h
        return pltpu.make_async_remote_copy(
            src_ref=source, dst_ref=tok.at[slot * 2 + h], send_sem=ag_send.at[m],
            recv_sem=ag_recv.at[m], device_id=target, device_id_type=pl.DeviceIdType.MESH,
        )

    gather = {}
    for h in range(2):
        mine = tokens_ref.at[:, pl.ds(h * half, half)]
        gather[1, h] = message(1, h, mine, up)
        gather[2, h] = message(2, h, mine, dn)
        gather[3, h] = message(3, h, mine, over)
        gather[5, h] = message(5, h, tok.at[6 + h], up)
        gather[6, h] = message(6, h, tok.at[6 + h], dn)
        gather[7, h] = message(7, h, tok.at[8 + h], over)
    gather[4, 0] = message(4, 0, tok.at[2], up)
    gather[4, 1] = message(4, 1, tok.at[5], dn)
    for key in ((1, 0), (2, 1), (3, 0), (1, 1), (2, 0), (3, 1)):
        gather[key].start()

    per_rows = block // rows

    def taps_copy(d):
        peer = (me + d) % nctx
        return pltpu.make_async_remote_copy(
            src_ref=taps_t.at[pl.ds(pl.multiple_of(peer * chans, chans), chans), :],
            dst_ref=ft.at[me // per_rows, :, pl.ds(pl.multiple_of((me % per_rows) * rows, rows), rows)],
            send_sem=ft_send.at[d], recv_sem=ft_recv.at[d],
            device_id={"ctx": peer}, device_id_type=pl.DeviceIdType.MESH,
        )

    def start_taps(d, c):
        taps_copy(d).start()
        return c

    lax.fori_loop(1, nctx, start_taps, 0)
    own_taps = pltpu.make_async_copy(
        taps_t.at[pl.ds(pl.multiple_of(me * chans, chans), chans), :],
        ft.at[me // per_rows, :, pl.ds(pl.multiple_of((me % per_rows) * rows, rows), rows)],
        own_sem.at[0],
    )
    own_taps.start()

    def invert(j, c):
        found = jnp.int32(0)
        for s in range(blocks):
            found = jnp.where(order_ref[s] == j, jnp.int32(s), found)
        inv_ref[j] = found
        return c

    def project(slot, h, streams, first=False):
        index = slot * 2 + h
        left = tok[index]
        for k in streams:
            value = jnp.dot(left, wv[index, k], preferred_element_type=F32)
            if first:
                acc[k] = value
            else:
                acc[k] += value

    forwards = {
        (1, 0): ((4, 0),), (2, 1): ((4, 1),), (3, 0): ((5, 0), (6, 0)), (3, 1): ((5, 1), (6, 1)),
        (4, 0): ((7, 0),), (4, 1): ((7, 1),),
    }
    for step, (slot, h) in enumerate(GATHER_ORDER):
        if slot == 0:
            own_load(h).wait()
        else:
            gather[slot, h].wait_recv()
            for key in forwards.get((slot, h), ()):
                gather[key].start()
        w_load(slot, h).wait()
        last = step == len(GATHER_ORDER) - 1
        project(slot, h, (0, 2) if last else (0, 1, 2), first=step == 0)
        if step == 1:
            lax.fori_loop(0, blocks, invert, 0)
        if step == 8:
            own_taps.wait()

            def wait_taps(d, c):
                taps_copy(d).wait_recv()
                return c

            lax.fori_loop(1, nctx, wait_taps, 0)
            tab_f_load.wait()
            lane = lax.broadcasted_iota(jnp.int32, (chans, block), 1)
            sign = jnp.where(lane % 2 == 0, 1.0, -1.0).astype(F32)
            before_r = jnp.zeros((chans, block), F32)
            before_i = jnp.zeros((chans, block), F32)
            for j in range(long_blocks):
                spectrum = jnp.dot(ft[j], tab_f[...], preferred_element_type=F32)
                now_r, now_i = spectrum[:, :block], spectrum[:, block:]
                real = before_r + sign * now_r
                imag = before_i + sign * now_i
                fr[j] = real
                fi[j] = jnp.where(lane == 0, 0.0, imag)
                fz[j] = jnp.where(lane == 0, imag, real)
                before_r, before_i = now_r, now_i

    for c in range(0, width, 128):
        for b in range(held):
            at = slice(b * block_len, (b + 1) * block_len)
            first = acc[0, at, c : c + 128].astype(BF16).astype(F32)
            third = acc[2, at, c : c + 128].astype(BF16).astype(F32)
            mt[b, c : c + 128, :] = (first * third).T.astype(BF16)

    def mixed_copy(d):
        peer = (me + d) % nctx
        return pltpu.make_async_remote_copy(
            src_ref=mt.at[:, pl.ds(pl.multiple_of(peer * chans, chans), chans), :],
            dst_ref=mx.at[pl.ds(me * held, held)],
            send_sem=mx_send.at[d], recv_sem=mx_recv.at[d],
            device_id={"ctx": peer}, device_id_type=pl.DeviceIdType.MESH,
        )

    def start_mixed(d, c):
        mixed_copy(d).start()
        return c

    lax.fori_loop(1, nctx, start_mixed, 0)
    own_mixed = pltpu.make_async_copy(
        mt.at[:, pl.ds(pl.multiple_of(me * chans, chans), chans), :],
        mx.at[pl.ds(me * held, held)], own_sem.at[1],
    )
    own_mixed.start()

    project(7, 1, (1,))
    for c in range(0, width, 128):
        for b in range(held):
            at = slice(b * block_len, (b + 1) * block_len)
            p1t[b, c : c + 128, :] = acc[1, at, c : c + 128].T.astype(BF16)
    tab_i_load.wait()

    own_mixed.wait()

    def wait_mixed(d, c):
        mixed_copy(d).wait_recv()
        return c

    lax.fori_loop(1, nctx, wait_mixed, 0)

    for j in range(blocks):
        at = (j % per_long) * block_len
        xn[j // per_long, :, at : at + block_len] = mx[inv_ref[j]]
    count = long_blocks * chans
    spectra = jnp.dot(xn[...].reshape(count, block), tab_f[...], preferred_element_type=F32)
    sp[...] = spectra.reshape(long_blocks, chans, 2 * block)

    lane_tiles = block // 128

    def products(tile, c):
        r0 = pl.multiple_of((tile // lane_tiles) * 8, 8)
        f0 = pl.multiple_of((tile % lane_tiles) * 128, 128)
        at = (pl.ds(r0, 8), pl.ds(f0, 128))
        at_i = (pl.ds(r0, 8), pl.ds(block + f0, 128))
        data_r = [sp[(j,) + at] for j in range(long_blocks)]
        data_i = [sp[(j,) + at_i] for j in range(long_blocks)]
        filt_r = [fr[(j,) + at] for j in range(long_blocks)]
        filt_i = [fi[(j,) + at] for j in range(long_blocks)]
        filt_z = [fz[(j,) + at] for j in range(long_blocks)]
        for i in range(long_blocks):
            total_r = data_r[0] * filt_r[i] - data_i[0] * filt_i[i]
            total_i = data_r[0] * filt_i[i] + data_i[0] * filt_z[i]
            for j in range(1, i + 1):
                total_r = total_r + (data_r[j] * filt_r[i - j] - data_i[j] * filt_i[i - j])
                total_i = total_i + (data_r[j] * filt_i[i - j] + data_i[j] * filt_z[i - j])
            tot[(i,) + at] = total_r
            tot[(i,) + at_i] = total_i
        return c

    lax.fori_loop(0, (chans // 8) * lane_tiles, products, 0)
    result = jnp.dot(
        tot[...].reshape(count, 2 * block).astype(BF16), tab_i[...], preferred_element_type=F32
    ).astype(BF16)
    for j in range(blocks):
        at = (j % per_long) * block_len
        r0 = (j // per_long) * chans
        yn[j] = result[r0 : r0 + chans, at : at + block_len]
    for s in range(blocks):
        ys[s] = yn[order_ref[s]]

    def back_copy(d):
        peer = (me + d) % nctx
        return pltpu.make_async_remote_copy(
            src_ref=ys.at[pl.ds(peer * held, held)],
            dst_ref=yr.at[:, pl.ds(pl.multiple_of(me * chans, chans), chans), :],
            send_sem=yr_send.at[d], recv_sem=yr_recv.at[d],
            device_id={"ctx": peer}, device_id_type=pl.DeviceIdType.MESH,
        )

    def start_back(d, c):
        back_copy(d).start()
        return c

    lax.fori_loop(1, nctx, start_back, 0)
    own_back = pltpu.make_async_copy(
        ys.at[pl.ds(me * held, held)],
        yr.at[:, pl.ds(pl.multiple_of(me * chans, chans), chans), :], own_sem.at[2],
    )
    own_back.start()
    for slot in range(8):
        for h in range(2):
            wo_load(slot, h).wait()
    own_back.wait()

    def wait_back(d, c):
        back_copy(d).wait_recv()
        return c

    lax.fori_loop(1, nctx, wait_back, 0)

    for b in range(held):
        for c in range(0, width, 128):
            value = p1t[b, c : c + 128, :].astype(F32) * yr[b, c : c + 128, :].astype(F32)
            gated[b * block_len : (b + 1) * block_len, c : c + 128] = value.T.astype(BF16)

    def out_part(slot, h):
        return jnp.dot(gated[...], wo[slot * 2 + h], preferred_element_type=F32)

    targets = {"a": over, "bu": up, "bd": dn, "c": None, "d": over, "eu": up, "ed": dn}
    places = {
        ("a", 0): 0, ("a", 1): 1, ("bu", 0): 2, ("bu", 1): 3, ("bd", 0): 4, ("bd", 1): 5,
        ("c", 0): 6, ("c", 1): 7, ("d", 0): 8, ("d", 1): 9, ("eu", 0): 10, ("eu", 1): 11,
        ("ed", 0): 12, ("ed", 1): 13,
    }

    def rs_copy(name, h):
        m = places[name, h]
        target = targets[name]
        if name == "c":
            target = up if h == 0 else dn
        return pltpu.make_async_remote_copy(
            src_ref=rout.at[m], dst_ref=rin.at[m], send_sem=rs_send.at[m], recv_sem=rs_recv.at[m],
            device_id=target, device_id_type=pl.DeviceIdType.MESH,
        )

    def send(name, h, value):
        rout[places[name, h]] = value.astype(BF16)
        rs_copy(name, h).start()

    def receive(name, h):
        rs_copy(name, h).wait_recv()
        return rin[places[name, h]].astype(F32)

    for name, slot, h in (
        ("a", 7, 0), ("bu", 6, 0), ("bd", 5, 1), ("a", 7, 1), ("bu", 6, 1), ("bd", 5, 0),
    ):
        send(name, h, out_part(slot, h))
    for slot in range(5):
        for h in range(2):
            part[slot * 2 + h] = out_part(slot, h)
    send("c", 0, part[8] + receive("a", 0))
    send("c", 1, part[9] + receive("a", 1))
    send("eu", 1, part[5])
    send("ed", 0, part[2])
    for h in range(2):
        send("d", h, part[6 + h] + receive("bu", h) + receive("bd", h))
    send("eu", 0, part[4] + receive("c", 0))
    send("ed", 1, part[3] + receive("c", 1))
    for h in range(2):
        total = part[h] + receive("d", h)
        total = total + receive("eu", h) + receive("ed", h)
        out_ref[:, h * half : (h + 1) * half] = total.astype(BF16)

    for key in gather:
        gather[key].wait_send()

    def drain(d, c):
        taps_copy(d).wait_send()
        mixed_copy(d).wait_send()
        back_copy(d).wait_send()
        return c

    lax.fori_loop(1, nctx, drain, 0)
    for name, h in places:
        rs_copy(name, h).wait_send()


def local(nctx, nch, block, tokens, filter_taps, block_order, in_weights, out_weights):
    rows, width = tokens.shape
    blocks = block_order.shape[0]
    block_len = rows * nctx // blocks
    half = width // 2
    chans = width // nctx
    held = rows // block_len
    long_blocks = rows * nctx // block
    forward, inverse = spectral_tables(block)
    dims = (nctx, nch, rows, width, block_len, block)
    hbm = pl.BlockSpec(memory_space=pl.ANY)
    dma = pltpu.SemaphoreType.DMA
    return pl.pallas_call(
        functools.partial(kernel, dims),
        out_shape=jax.ShapeDtypeStruct((rows, width), BF16),
        in_specs=[pl.BlockSpec(memory_space=pltpu.SMEM)] + [hbm] * 6,
        out_specs=pl.BlockSpec(memory_space=pltpu.VMEM),
        scratch_shapes=[
            pltpu.VMEM((16, rows, half), BF16),
            pltpu.VMEM((16, 3, half, width), BF16),
            pltpu.VMEM((16, width, half), BF16),
            pltpu.VMEM((3, rows, width), F32),
            pltpu.VMEM(forward.shape, BF16),
            pltpu.VMEM(inverse.shape, BF16),
            pltpu.VMEM((rows, width), BF16),
            pltpu.VMEM((width, rows), BF16),
            pltpu.VMEM((long_blocks, chans, block), BF16),
            pltpu.VMEM((long_blocks, chans, block), F32),
            pltpu.VMEM((long_blocks, chans, block), F32),
            pltpu.VMEM((long_blocks, chans, block), F32),
            pltpu.VMEM((held, width, block_len), BF16),
            pltpu.VMEM((blocks, chans, block_len), BF16),
            pltpu.VMEM((long_blocks, chans, block), BF16),
            pltpu.VMEM((long_blocks, chans, 2 * block), F32),
            pltpu.VMEM((long_blocks, chans, 2 * block), F32),
            pltpu.VMEM((blocks, chans, block_len), BF16),
            pltpu.VMEM((blocks, chans, block_len), BF16),
            pltpu.VMEM((held, width, block_len), BF16),
            pltpu.VMEM((held, width, block_len), BF16),
            pltpu.VMEM((rows, width), BF16),
            pltpu.VMEM((10, rows, half), F32),
            pltpu.VMEM((14, rows, half), BF16),
            pltpu.VMEM((14, rows, half), BF16),
            pltpu.SMEM((blocks,), jnp.int32),
            dma((5,)), dma((16,)), dma((16,)),
            dma((14,)), dma((14,)),
            dma((nctx,)), dma((nctx,)),
            dma((nctx,)), dma((nctx,)),
            dma((nctx,)), dma((nctx,)),
            dma((14,)), dma((14,)),
            dma((3,)),
        ],
        compiler_params=pltpu.CompilerParams(
            collective_id=0, has_side_effects=True, vmem_limit_bytes=56 * 2**20
        ),
        name="hyena_layer",
    )(block_order, tokens, filter_taps, in_weights, out_weights, jnp.asarray(forward), jnp.asarray(inverse))


def solution(mesh):
    placed = (P("ctx", "ch"), P("ctx", "ch"), P(), P(None, None, "ch"), P("ch", None))
    body = functools.partial(local, mesh.shape["ctx"], mesh.shape["ch"], 512)
    return jax.shard_map(body, mesh=mesh, in_specs=placed, out_specs=P("ctx", "ch"), check_vma=False)
```

```python
import functools
import math

import jax
import jax.numpy as jnp
import ml_dtypes
import numpy as np
from jax import lax
from jax.experimental import pallas as pl
from jax.experimental.pallas import tpu as pltpu
from jax.sharding import PartitionSpec as P

F32 = jnp.float32
BF16 = jnp.bfloat16


def spectral_tables(block):
    length = 2 * block
    index = np.arange(block)
    angles = 2.0 * math.pi * ((index[:, None] * index[None, :]) % length) / length
    real, imag = np.cos(angles), -np.sin(angles)
    imag[:, 0] = 1.0 - 2.0 * (index % 2)
    forward = np.concatenate([real, imag], 1).astype(ml_dtypes.bfloat16)
    later = index + block
    back = 2.0 * math.pi * ((index[:, None] * later[None, :]) % length) / length
    real, imag = 2.0 * np.cos(back) / length, -2.0 * np.sin(back) / length
    real[0] = 1.0 / length
    imag[0] = (1.0 - 2.0 * (later % 2)) / length
    inverse = np.concatenate([real, imag], 0).astype(ml_dtypes.bfloat16)
    return forward, inverse


GATHER_ORDER = (
    (0, 0), (0, 1), (1, 0), (2, 1), (3, 0), (1, 1), (2, 0), (3, 1),
    (4, 0), (4, 1), (5, 0), (6, 0), (7, 0), (5, 1), (6, 1), (7, 1),
)


def kernel(
    dims, order_ref, tokens_ref, taps_ref, w_in_ref, w_out_ref, tab_f_ref, tab_i_ref, out_ref,
    tok, wv, wo, acc, tab_f, tab_i, taps_v, taps_t, ft, fr, fi, fz, mt, mx, xn, sp, tot, yn, ys, yr,
    p1t, gated, part, rin, rout, inv_ref,
    load_sem, w_sem, wo_sem, ag_send, ag_recv, ft_send, ft_recv, mx_send, mx_recv, yr_send, yr_recv,
    rs_send, rs_recv, own_sem,
):
    nctx, nch, rows, width, block_len, block = dims
    half = width // 2
    ny = nch // 2
    chans = width // nctx
    blocks = nctx * rows // block_len
    held = rows // block_len
    long_blocks = nctx * rows // block
    per_long = block // block_len
    near = sorted(range(1, nctx), key=lambda d: min(d, nctx - d))
    me = lax.axis_index("ctx")
    ch = lax.axis_index("ch")
    z = ch // ny
    y = ch % ny
    zo = 1 - z
    y_up = (y + 1) % ny
    y_dn = (y + ny - 1) % ny
    y_far = (y + 2) % ny
    up = {"ch": z * ny + y_up}
    dn = {"ch": z * ny + y_dn}
    over = {"ch": zo * ny + y}
    shard_of = (
        z * ny + y, z * ny + y_dn, z * ny + y_up, zo * ny + y,
        z * ny + y_far, zo * ny + y_dn, zo * ny + y_up, zo * ny + y_far,
    )

    def own_load(h):
        return pltpu.make_async_copy(
            tokens_ref.at[:, pl.ds(h * half, half)], tok.at[h], load_sem.at[h]
        )

    def w_load(slot, h):
        start = pl.multiple_of(shard_of[slot] * width + h * half, half)
        return pltpu.make_async_copy(
            w_in_ref.at[:, pl.ds(start, half), :], wv.at[slot * 2 + h], w_sem.at[slot * 2 + h]
        )

    def wo_load(slot, h):
        start = pl.multiple_of(shard_of[slot] * width + h * half, half)
        return pltpu.make_async_copy(
            w_out_ref.at[:, pl.ds(start, half)], wo.at[slot * 2 + h], wo_sem.at[slot * 2 + h]
        )

    taps_load = pltpu.make_async_copy(taps_ref, taps_v, load_sem.at[2])
    tab_f_load = pltpu.make_async_copy(tab_f_ref, tab_f, load_sem.at[3])
    tab_i_load = pltpu.make_async_copy(tab_i_ref, tab_i, load_sem.at[4])
    barrier = pltpu.get_barrier_semaphore()
    for neighbour in (up, dn, over):
        pl.semaphore_signal(barrier, inc=1, device_id=neighbour, device_id_type=pl.DeviceIdType.MESH)

    def greet(d, c):
        pl.semaphore_signal(
            barrier, inc=1, device_id={"ctx": (me + d) % nctx}, device_id_type=pl.DeviceIdType.MESH
        )
        return c

    lax.fori_loop(1, nctx, greet, 0)

    taps_load.start()
    own_load(0).start()
    own_load(1).start()
    pl.semaphore_wait(barrier, 3 + nctx - 1)

    def message(slot, h, source, target):
        m = (slot - 1) * 2 + h
        return pltpu.make_async_remote_copy(
            src_ref=source, dst_ref=tok.at[slot * 2 + h], send_sem=ag_send.at[m],
            recv_sem=ag_recv.at[m], device_id=target, device_id_type=pl.DeviceIdType.MESH,
        )

    gather = {}
    for h in range(2):
        mine = tokens_ref.at[:, pl.ds(h * half, half)]
        gather[1, h] = message(1, h, mine, up)
        gather[2, h] = message(2, h, mine, dn)
        gather[3, h] = message(3, h, mine, over)
        gather[5, h] = message(5, h, tok.at[6 + h], up)
        gather[6, h] = message(6, h, tok.at[6 + h], dn)
        gather[7, h] = message(7, h, tok.at[8 + h], over)
    gather[4, 0] = message(4, 0, tok.at[2], up)
    gather[4, 1] = message(4, 1, tok.at[5], dn)
    for key in ((1, 0), (2, 1), (3, 0), (1, 1), (2, 0), (3, 1)):
        gather[key].start()

    for slot, h in GATHER_ORDER[:8]:
        w_load(slot, h).start()
    tab_f_load.start()
    for slot, h in GATHER_ORDER[8:]:
        w_load(slot, h).start()
    tab_i_load.start()
    for slot in (7, 6, 5, 4, 3, 2, 1, 0):
        for h in range(2):
            wo_load(slot, h).start()

    taps_load.wait()
    for r in range(0, rows, 128):
        for c in range(0, width, 128):
            piece = taps_v[r : r + 128, c : c + 128].astype(F32)
            taps_t[c : c + 128, r : r + 128] = piece.T.astype(BF16)

    per_rows = block // rows

    def taps_copy(d):
        peer = (me + d) % nctx
        return pltpu.make_async_remote_copy(
            src_ref=taps_t.at[pl.ds(pl.multiple_of(peer * chans, chans), chans), :],
            dst_ref=ft.at[me // per_rows, :, pl.ds(pl.multiple_of((me % per_rows) * rows, rows), rows)],
            send_sem=ft_send.at[d], recv_sem=ft_recv.at[d],
            device_id={"ctx": peer}, device_id_type=pl.DeviceIdType.MESH,
        )

    def start_taps(d, c):
        taps_copy(d).start()
        return c

    lax.fori_loop(1, nctx, start_taps, 0)
    own_taps = pltpu.make_async_copy(
        taps_t.at[pl.ds(pl.multiple_of(me * chans, chans), chans), :],
        ft.at[me // per_rows, :, pl.ds(pl.multiple_of((me % per_rows) * rows, rows), rows)],
        own_sem.at[0],
    )
    own_taps.start()

    def invert(j, c):
        found = jnp.int32(0)
        for s in range(blocks):
            found = jnp.where(order_ref[s] == j, jnp.int32(s), found)
        inv_ref[j] = found
        return c

    def project(slot, h, streams, first=False):
        index = slot * 2 + h
        left = tok[index]
        for k in streams:
            value = jnp.dot(left, wv[index, k], preferred_element_type=F32)
            if first:
                acc[k] = value
            else:
                acc[k] += value

    forwards = {
        (1, 0): ((4, 0),), (2, 1): ((4, 1),), (3, 0): ((5, 0), (6, 0)), (3, 1): ((5, 1), (6, 1)),
        (4, 0): ((7, 0),), (4, 1): ((7, 1),),
    }
    for step, (slot, h) in enumerate(GATHER_ORDER):
        if slot == 0:
            own_load(h).wait()
        else:
            gather[slot, h].wait_recv()
            for key in forwards.get((slot, h), ()):
                gather[key].start()
        w_load(slot, h).wait()
        last = step == len(GATHER_ORDER) - 1
        project(slot, h, (0, 2) if last else (0, 1, 2), first=step == 0)
        if step == 1:
            lax.fori_loop(0, blocks, invert, 0)
        if step == 8:
            own_taps.wait()

            def wait_taps(d, c):
                taps_copy(d).wait_recv()
                return c

            lax.fori_loop(1, nctx, wait_taps, 0)
            tab_f_load.wait()
            lane = lax.broadcasted_iota(jnp.int32, (chans, block), 1)
            sign = jnp.where(lane % 2 == 0, 1.0, -1.0).astype(F32)
            before_r = jnp.zeros((chans, block), F32)
            before_i = jnp.zeros((chans, block), F32)
            for j in range(long_blocks):
                spectrum = jnp.dot(ft[j], tab_f[...], preferred_element_type=F32)
                now_r, now_i = spectrum[:, :block], spectrum[:, block:]
                real = before_r + sign * now_r
                imag = before_i + sign * now_i
                fr[j] = real
                fi[j] = jnp.where(lane == 0, 0.0, imag)
                fz[j] = jnp.where(lane == 0, imag, real)
                before_r, before_i = now_r, now_i

    for c in range(0, width, 128):
        for b in range(held):
            at = slice(b * block_len, (b + 1) * block_len)
            first = acc[0, at, c : c + 128].astype(BF16).astype(F32)
            third = acc[2, at, c : c + 128].astype(BF16).astype(F32)
            mt[b, c : c + 128, :] = (first * third).T.astype(BF16)

    def mixed_copy(d):
        peer = (me + d) % nctx
        return pltpu.make_async_remote_copy(
            src_ref=mt.at[:, pl.ds(pl.multiple_of(peer * chans, chans), chans), :],
            dst_ref=mx.at[pl.ds(me * held, held)],
            send_sem=mx_send.at[d], recv_sem=mx_recv.at[d],
            device_id={"ctx": peer}, device_id_type=pl.DeviceIdType.MESH,
        )

    for d in near:
        mixed_copy(d).start()
    own_mixed = pltpu.make_async_copy(
        mt.at[:, pl.ds(pl.multiple_of(me * chans, chans), chans), :],
        mx.at[pl.ds(me * held, held)], own_sem.at[1],
    )
    own_mixed.start()

    project(7, 1, (1,))
    for c in range(0, width, 128):
        for b in range(held):
            at = slice(b * block_len, (b + 1) * block_len)
            p1t[b, c : c + 128, :] = acc[1, at, c : c + 128].T.astype(BF16)
    tab_i_load.wait()

    own_mixed.wait()

    for d in near:
        mixed_copy(d).wait_recv()

    for j in range(blocks):
        at = (j % per_long) * block_len
        xn[j // per_long, :, at : at + block_len] = mx[inv_ref[j]]
    count = long_blocks * chans
    spectra = jnp.dot(xn[...].reshape(count, block), tab_f[...], preferred_element_type=F32)
    sp[...] = spectra.reshape(long_blocks, chans, 2 * block)

    lane_tiles = block // 128

    def products(tile, c):
        r0 = pl.multiple_of((tile // lane_tiles) * 8, 8)
        f0 = pl.multiple_of((tile % lane_tiles) * 128, 128)
        at = (pl.ds(r0, 8), pl.ds(f0, 128))
        at_i = (pl.ds(r0, 8), pl.ds(block + f0, 128))
        data_r = [sp[(j,) + at] for j in range(long_blocks)]
        data_i = [sp[(j,) + at_i] for j in range(long_blocks)]
        filt_r = [fr[(j,) + at] for j in range(long_blocks)]
        filt_i = [fi[(j,) + at] for j in range(long_blocks)]
        filt_z = [fz[(j,) + at] for j in range(long_blocks)]
        for i in range(long_blocks):
            total_r = data_r[0] * filt_r[i] - data_i[0] * filt_i[i]
            total_i = data_r[0] * filt_i[i] + data_i[0] * filt_z[i]
            for j in range(1, i + 1):
                total_r = total_r + (data_r[j] * filt_r[i - j] - data_i[j] * filt_i[i - j])
                total_i = total_i + (data_r[j] * filt_i[i - j] + data_i[j] * filt_z[i - j])
            tot[(i,) + at] = total_r
            tot[(i,) + at_i] = total_i
        return c

    lax.fori_loop(0, (chans // 8) * lane_tiles, products, 0)
    result = jnp.dot(
        tot[...].reshape(count, 2 * block).astype(BF16), tab_i[...], preferred_element_type=F32
    ).astype(BF16)
    for j in range(blocks):
        at = (j % per_long) * block_len
        r0 = (j // per_long) * chans
        yn[j] = result[r0 : r0 + chans, at : at + block_len]
    for s in range(blocks):
        ys[s] = yn[order_ref[s]]

    def back_copy(d):
        peer = (me + d) % nctx
        return pltpu.make_async_remote_copy(
            src_ref=ys.at[pl.ds(peer * held, held)],
            dst_ref=yr.at[:, pl.ds(pl.multiple_of(me * chans, chans), chans), :],
            send_sem=yr_send.at[d], recv_sem=yr_recv.at[d],
            device_id={"ctx": peer}, device_id_type=pl.DeviceIdType.MESH,
        )

    for d in near:
        back_copy(d).start()
    own_back = pltpu.make_async_copy(
        ys.at[pl.ds(me * held, held)],
        yr.at[:, pl.ds(pl.multiple_of(me * chans, chans), chans), :], own_sem.at[2],
    )
    own_back.start()
    for slot in range(8):
        for h in range(2):
            wo_load(slot, h).wait()
    own_back.wait()

    for d in near:
        back_copy(d).wait_recv()

    for b in range(held):
        for c in range(0, width, 128):
            value = p1t[b, c : c + 128, :].astype(F32) * yr[b, c : c + 128, :].astype(F32)
            gated[b * block_len : (b + 1) * block_len, c : c + 128] = value.T.astype(BF16)

    def out_part(slot, h):
        return jnp.dot(gated[...], wo[slot * 2 + h], preferred_element_type=F32)

    targets = {"a": over, "bu": up, "bd": dn, "c": None, "d": over, "eu": up, "ed": dn}
    places = {
        ("a", 0): 0, ("a", 1): 1, ("bu", 0): 2, ("bu", 1): 3, ("bd", 0): 4, ("bd", 1): 5,
        ("c", 0): 6, ("c", 1): 7, ("d", 0): 8, ("d", 1): 9, ("eu", 0): 10, ("eu", 1): 11,
        ("ed", 0): 12, ("ed", 1): 13,
    }

    def rs_copy(name, h):
        m = places[name, h]
        target = targets[name]
        if name == "c":
            target = up if h == 0 else dn
        return pltpu.make_async_remote_copy(
            src_ref=rout.at[m], dst_ref=rin.at[m], send_sem=rs_send.at[m], recv_sem=rs_recv.at[m],
            device_id=target, device_id_type=pl.DeviceIdType.MESH,
        )

    def send(name, h, value):
        rout[places[name, h]] = value.astype(BF16)
        rs_copy(name, h).start()

    def receive(name, h):
        rs_copy(name, h).wait_recv()
        return rin[places[name, h]].astype(F32)

    for name, slot, h in (
        ("a", 7, 0), ("bu", 6, 0), ("bd", 5, 1), ("a", 7, 1), ("bu", 6, 1), ("bd", 5, 0),
    ):
        send(name, h, out_part(slot, h))
    for slot in range(5):
        for h in range(2):
            part[slot * 2 + h] = out_part(slot, h)
    send("c", 0, part[8] + receive("a", 0))
    send("c", 1, part[9] + receive("a", 1))
    send("eu", 1, part[5])
    send("ed", 0, part[2])
    for h in range(2):
        send("d", h, part[6 + h] + receive("bu", h) + receive("bd", h))
    send("eu", 0, part[4] + receive("c", 0))
    send("ed", 1, part[3] + receive("c", 1))
    for h in range(2):
        total = part[h] + receive("d", h)
        total = total + receive("eu", h) + receive("ed", h)
        out_ref[:, h * half : (h + 1) * half] = total.astype(BF16)

    for key in gather:
        gather[key].wait_send()

    def drain(d, c):
        taps_copy(d).wait_send()
        mixed_copy(d).wait_send()
        back_copy(d).wait_send()
        return c

    lax.fori_loop(1, nctx, drain, 0)
    for name, h in places:
        rs_copy(name, h).wait_send()


def local(nctx, nch, block, tokens, filter_taps, block_order, in_weights, out_weights):
    rows, width = tokens.shape
    blocks = block_order.shape[0]
    block_len = rows * nctx // blocks
    half = width // 2
    chans = width // nctx
    held = rows // block_len
    long_blocks = rows * nctx // block
    forward, inverse = spectral_tables(block)
    dims = (nctx, nch, rows, width, block_len, block)
    hbm = pl.BlockSpec(memory_space=pl.ANY)
    dma = pltpu.SemaphoreType.DMA
    return pl.pallas_call(
        functools.partial(kernel, dims),
        out_shape=pltpu.VMEM((rows, width), BF16),
        in_specs=[pl.BlockSpec(memory_space=pltpu.SMEM)] + [hbm] * 6,
        out_specs=pl.BlockSpec(memory_space=pltpu.VMEM),
        scratch_shapes=[
            pltpu.VMEM((16, rows, half), BF16),
            pltpu.VMEM((16, 3, half, width), BF16),
            pltpu.VMEM((16, width, half), BF16),
            pltpu.VMEM((3, rows, width), F32),
            pltpu.VMEM(forward.shape, BF16),
            pltpu.VMEM(inverse.shape, BF16),
            pltpu.VMEM((rows, width), BF16),
            pltpu.VMEM((width, rows), BF16),
            pltpu.VMEM((long_blocks, chans, block), BF16),
            pltpu.VMEM((long_blocks, chans, block), F32),
            pltpu.VMEM((long_blocks, chans, block), F32),
            pltpu.VMEM((long_blocks, chans, block), F32),
            pltpu.VMEM((held, width, block_len), BF16),
            pltpu.VMEM((blocks, chans, block_len), BF16),
            pltpu.VMEM((long_blocks, chans, block), BF16),
            pltpu.VMEM((long_blocks, chans, 2 * block), F32),
            pltpu.VMEM((long_blocks, chans, 2 * block), F32),
            pltpu.VMEM((blocks, chans, block_len), BF16),
            pltpu.VMEM((blocks, chans, block_len), BF16),
            pltpu.VMEM((held, width, block_len), BF16),
            pltpu.VMEM((held, width, block_len), BF16),
            pltpu.VMEM((rows, width), BF16),
            pltpu.VMEM((10, rows, half), F32),
            pltpu.VMEM((14, rows, half), BF16),
            pltpu.VMEM((14, rows, half), BF16),
            pltpu.SMEM((blocks,), jnp.int32),
            dma((5,)), dma((16,)), dma((16,)),
            dma((14,)), dma((14,)),
            dma((nctx,)), dma((nctx,)),
            dma((nctx,)), dma((nctx,)),
            dma((nctx,)), dma((nctx,)),
            dma((14,)), dma((14,)),
            dma((3,)),
        ],
        compiler_params=pltpu.CompilerParams(
            collective_id=0, has_side_effects=True, vmem_limit_bytes=56 * 2**20
        ),
        name="hyena_layer",
    )(block_order, tokens, filter_taps, in_weights, out_weights, jnp.asarray(forward), jnp.asarray(inverse))


def solution(mesh):
    placed = (P("ctx", "ch"), P("ctx", "ch"), P(), P(None, None, "ch"), P("ch", None))
    body = functools.partial(local, mesh.shape["ctx"], mesh.shape["ch"], 512)
    return jax.shard_map(body, mesh=mesh, in_specs=placed, out_specs=P("ctx", "ch"), check_vma=False)
```

```python
import functools
import math

import jax
import jax.numpy as jnp
import ml_dtypes
import numpy as np
from jax import lax
from jax.experimental import pallas as pl
from jax.experimental.pallas import tpu as pltpu
from jax.sharding import PartitionSpec as P

F32 = jnp.float32
BF16 = jnp.bfloat16


def spectral_tables(block):
    length = 2 * block
    index = np.arange(block)
    angles = 2.0 * math.pi * ((index[:, None] * index[None, :]) % length) / length
    real, imag = np.cos(angles), -np.sin(angles)
    imag[:, 0] = 1.0 - 2.0 * (index % 2)
    forward = np.concatenate([real, imag], 1).astype(ml_dtypes.bfloat16)
    later = index + block
    back = 2.0 * math.pi * ((index[:, None] * later[None, :]) % length) / length
    real, imag = 2.0 * np.cos(back) / length, -2.0 * np.sin(back) / length
    real[0] = 1.0 / length
    imag[0] = (1.0 - 2.0 * (later % 2)) / length
    inverse = np.concatenate([real, imag], 0).astype(ml_dtypes.bfloat16)
    return forward, inverse


ARRIVALS = (
    (1, 0), (2, 3), (1, 1), (2, 2), (3, 1), "p10", (3, 2), "p21", (1, 2), (2, 1), (3, 0), "p30", (1, 3), (2, 0),
    (3, 3), "p11", "p20", "p31", (4, 0), (4, 3), (4, 1), (4, 2), "p40", "p41", "filter",
    (5, 0), (5, 1), "p50", (6, 3), (6, 2), "p61", (5, 2), (5, 3), "p51", (6, 1), (6, 0), "p60",
    (7, 0), (7, 1), "p70", (7, 2), (7, 3), "p71",
)
FORWARDS = {
    (1, 0): ((4, 0), (5, 0)), (1, 1): ((4, 1),), (2, 3): ((4, 3), (6, 3)), (2, 2): ((4, 2),),
    (3, 0): ((6, 0),), (3, 1): ((5, 1), (6, 1)), (3, 2): ((5, 2), (6, 2)), (3, 3): ((5, 3),),
    (4, 0): ((7, 0),), (4, 1): ((7, 1),), (4, 2): ((7, 2),), (4, 3): ((7, 3),),
}


def kernel(
    dims, order_ref, tokens_ref, taps_ref, w_in_ref, w_out_ref, tab_f_ref, tab_i_ref, out_ref,
    tok, wv, wo, acc, tab_f, tab_i, taps_v, taps_t, ft, fr, fi, fz, mt, mx, xn, sp, tot, yn, ys, yr,
    p1t, gated, part, rin, rout, ord_ref, inv_ref,
    load_sem, w_sem, ag_send, ag_recv, ex_send, ex_recv, rs_send, rs_recv, own_sem,
):
    nctx, nch, rows, width, block_len, block = dims
    half = width // 2
    ny = nch // 2
    chans = width // nctx
    blocks = nctx * rows // block_len
    held = rows // block_len
    long_blocks = nctx * rows // block
    per_long = block // block_len
    near = sorted(range(1, nctx), key=lambda d: min(d, nctx - d))
    me = lax.axis_index("ctx")
    ch = lax.axis_index("ch")
    z = ch // ny
    y = ch % ny
    zo = 1 - z
    y_up = (y + 1) % ny
    y_dn = (y + ny - 1) % ny
    y_far = (y + 2) % ny
    up = {"ch": z * ny + y_up}
    dn = {"ch": z * ny + y_dn}
    over = {"ch": zo * ny + y}
    shard_of = (
        z * ny + y, z * ny + y_dn, z * ny + y_up, zo * ny + y,
        z * ny + y_far, zo * ny + y_dn, zo * ny + y_up, zo * ny + y_far,
    )

    def wait_bytes(ref, sem):
        pltpu.make_async_copy(ref, ref, sem).wait()

    barrier = pltpu.get_barrier_semaphore()
    for neighbour in (up, dn, over):
        pl.semaphore_signal(barrier, inc=1, device_id=neighbour, device_id_type=pl.DeviceIdType.MESH)
    for d in near[::-1]:
        pl.semaphore_signal(
            barrier, inc=1, device_id={"ctx": (me + d) % nctx}, device_id_type=pl.DeviceIdType.MESH
        )
    pl.semaphore_wait(barrier, 3 + nctx - 1)

    quarter = rows // 2

    def chunk(slot, c):
        return tok.at[slot * 2 + c // 2, pl.ds((c % 2) * quarter, quarter)]

    def message(slot, c, source, target):
        if source is None:
            source = tokens_ref.at[pl.ds((c % 2) * quarter, quarter), pl.ds((c // 2) * half, half)]
        else:
            source = chunk(source, c)
        return pltpu.make_async_remote_copy(
            src_ref=source, dst_ref=chunk(slot, c), send_sem=ag_send.at[0],
            recv_sem=ag_recv.at[(slot - 1) * 4 + c], device_id=target,
            device_id_type=pl.DeviceIdType.MESH,
        )

    gather = {}
    for c in range(4):
        gather[1, c] = message(1, c, None, up)
        gather[2, c] = message(2, c, None, dn)
        gather[3, c] = message(3, c, None, over)
        gather[4, c] = message(4, c, 1, up) if c < 2 else message(4, c, 2, dn)
        gather[5, c] = message(5, c, 1, over) if c == 0 else message(5, c, 3, up)
        gather[6, c] = message(6, c, 2, over) if c == 3 else message(6, c, 3, dn)
        gather[7, c] = message(7, c, 4, over)
    for keys in zip(((1, 0), (1, 1), (1, 2), (1, 3)), ((2, 3), (2, 2), (2, 1), (2, 0)), ((3, 1), (3, 2), (3, 0), (3, 3))):
        for key in keys:
            gather[key].start()

    taps_load = pltpu.make_async_copy(taps_ref, taps_v, load_sem.at[0])
    tab_f_load = pltpu.make_async_copy(tab_f_ref, tab_f, load_sem.at[1])
    tab_i_load = pltpu.make_async_copy(tab_i_ref, tab_i, load_sem.at[2])
    order_load = pltpu.make_async_copy(order_ref, ord_ref, load_sem.at[3])
    w_group = (0, 1, 1, 1, 2, 2, 2, 2)
    taps_load.start()
    for h in range(2):
        pltpu.make_async_copy(tokens_ref.at[:, pl.ds(h * half, half)], tok.at[h], load_sem.at[4]).start()
    for slot in range(8):
        start = pl.multiple_of(shard_of[slot] * width, width)
        pltpu.make_async_copy(
            w_in_ref.at[:, pl.ds(start, width), :], wv.at[slot], w_sem.at[w_group[slot]]
        ).start()
        if slot == 3:
            tab_f_load.start()
            order_load.start()
    tab_i_load.start()
    for slot in range(8):
        start = pl.multiple_of(shard_of[slot] * width, width)
        pltpu.make_async_copy(
            w_out_ref.at[:, pl.ds(start, width)], wo.at[slot], w_sem.at[3]
        ).start()

    taps_load.wait()
    for r in range(0, rows, 128):
        for c in range(0, width, 128):
            piece = taps_v[r : r + 128, c : c + 128].astype(F32)
            taps_t[c : c + 128, r : r + 128] = piece.T.astype(BF16)

    per_rows = block // rows
    mine = pl.ds(pl.multiple_of(me * chans, chans), chans)
    my_lags = pl.ds(pl.multiple_of((me % per_rows) * rows, rows), rows)

    def channels_of(peer):
        return pl.ds(pl.multiple_of(peer * chans, chans), chans)

    def taps_copy(d):
        peer = (me + d) % nctx
        return pltpu.make_async_remote_copy(
            src_ref=taps_t.at[channels_of(peer), :], dst_ref=ft.at[me // per_rows, :, my_lags],
            send_sem=ex_send.at[0], recv_sem=ex_recv.at[0],
            device_id={"ctx": peer}, device_id_type=pl.DeviceIdType.MESH,
        )

    def start_taps(d, c):
        taps_copy(d).start()
        return c

    lax.fori_loop(1, nctx, start_taps, 0)
    own_taps = pltpu.make_async_copy(
        taps_t.at[mine, :], ft.at[me // per_rows, :, my_lags], own_sem.at[0]
    )
    own_taps.start()

    def invert(j, c):
        found = jnp.int32(0)
        for s in range(blocks):
            found = jnp.where(ord_ref[s] == j, jnp.int32(s), found)
        inv_ref[j] = found
        return c

    def project(slot, h, streams, first=False):
        left = tok[slot * 2 + h]
        for k in streams:
            value = jnp.dot(left, wv[slot, k, h * half : (h + 1) * half, :], preferred_element_type=F32)
            if first:
                acc[k] = value
            else:
                acc[k] += value

    def filter_spectra():
        own_taps.wait()
        wait_bytes(taps_t.at[pl.ds(0, width - chans), :], ex_recv.at[0])
        tab_f_load.wait()
        lane = lax.broadcasted_iota(jnp.int32, (chans, block), 1)
        sign = jnp.where(lane % 2 == 0, 1.0, -1.0).astype(F32)
        before_r = jnp.zeros((chans, block), F32)
        before_i = jnp.zeros((chans, block), F32)
        for j in range(long_blocks):
            spectrum = jnp.dot(ft[j], tab_f[...], preferred_element_type=F32)
            now_r, now_i = spectrum[:, :block], spectrum[:, block:]
            real = before_r + sign * now_r
            imag = before_i + sign * now_i
            fr[j] = real
            fi[j] = jnp.where(lane == 0, 0.0, imag)
            fz[j] = jnp.where(lane == 0, imag, real)
            before_r, before_i = now_r, now_i
        order_load.wait()
        lax.fori_loop(0, blocks, invert, 0)

    wait_bytes(tok.at[pl.ds(0, 2)], load_sem.at[4])
    wait_bytes(wv.at[pl.ds(0, 1)], w_sem.at[0])
    project(0, 0, (0, 1, 2), first=True)
    waited = 0
    for step in ("p01",) + ARRIVALS:
        if step == "filter":
            filter_spectra()
        elif isinstance(step, str):
            slot, h = int(step[1]), int(step[2])
            if w_group[slot] > waited:
                waited = w_group[slot]
                wait_bytes(wv.at[pl.ds(1, 3)] if waited == 1 else wv.at[pl.ds(4, 4)], w_sem.at[waited])
            project(slot, h, (0, 2) if step == ARRIVALS[-1] else (0, 1, 2))
        else:
            gather[step].wait_recv()
            for key in FORWARDS.get(step, ()):
                gather[key].start()

    for c in range(0, width, 128):
        for b in range(held):
            at = slice(b * block_len, (b + 1) * block_len)
            first = acc[0, at, c : c + 128].astype(BF16).astype(F32)
            third = acc[2, at, c : c + 128].astype(BF16).astype(F32)
            mt[b, c : c + 128, :] = (first * third).T.astype(BF16)

    def mixed_copy(d):
        peer = (me + d) % nctx
        return pltpu.make_async_remote_copy(
            src_ref=mt.at[:, channels_of(peer), :], dst_ref=mx.at[pl.ds(me * held, held)],
            send_sem=ex_send.at[1], recv_sem=ex_recv.at[1],
            device_id={"ctx": peer}, device_id_type=pl.DeviceIdType.MESH,
        )

    for d in near:
        mixed_copy(d).start()
    own_mixed = pltpu.make_async_copy(
        mt.at[:, mine, :], mx.at[pl.ds(me * held, held)], own_sem.at[1]
    )
    own_mixed.start()

    project(7, 1, (1,))
    for c in range(0, width, 128):
        for b in range(held):
            at = slice(b * block_len, (b + 1) * block_len)
            p1t[b, c : c + 128, :] = acc[1, at, c : c + 128].T.astype(BF16)
    tab_i_load.wait()

    own_mixed.wait()

    wait_bytes(mx.at[pl.ds(0, blocks - held)], ex_recv.at[1])

    for j in range(blocks):
        at = (j % per_long) * block_len
        xn[j // per_long, :, at : at + block_len] = mx[inv_ref[j]]
    count = long_blocks * chans
    spectra = jnp.dot(xn[...].reshape(count, block), tab_f[...], preferred_element_type=F32)
    sp[...] = spectra.reshape(long_blocks, chans, 2 * block)

    lane_tiles = block // 128

    def products(tile, c):
        r0 = pl.multiple_of((tile // lane_tiles) * 8, 8)
        f0 = pl.multiple_of((tile % lane_tiles) * 128, 128)
        at = (pl.ds(r0, 8), pl.ds(f0, 128))
        at_i = (pl.ds(r0, 8), pl.ds(block + f0, 128))
        data_r = [sp[(j,) + at] for j in range(long_blocks)]
        data_i = [sp[(j,) + at_i] for j in range(long_blocks)]
        filt_r = [fr[(j,) + at] for j in range(long_blocks)]
        filt_i = [fi[(j,) + at] for j in range(long_blocks)]
        filt_z = [fz[(j,) + at] for j in range(long_blocks)]
        for i in range(long_blocks):
            total_r = data_r[0] * filt_r[i] - data_i[0] * filt_i[i]
            total_i = data_r[0] * filt_i[i] + data_i[0] * filt_z[i]
            for j in range(1, i + 1):
                total_r = total_r + (data_r[j] * filt_r[i - j] - data_i[j] * filt_i[i - j])
                total_i = total_i + (data_r[j] * filt_i[i - j] + data_i[j] * filt_z[i - j])
            tot[(i,) + at] = total_r
            tot[(i,) + at_i] = total_i
        return c

    lax.fori_loop(0, (chans // 8) * lane_tiles, products, 0)
    result = jnp.dot(
        tot[...].reshape(count, 2 * block).astype(BF16), tab_i[...], preferred_element_type=F32
    ).astype(BF16)
    for j in range(blocks):
        at = (j % per_long) * block_len
        r0 = (j // per_long) * chans
        yn[j] = result[r0 : r0 + chans, at : at + block_len]
    for s in range(blocks):
        ys[s] = yn[ord_ref[s]]

    def back_copy(d):
        peer = (me + d) % nctx
        return pltpu.make_async_remote_copy(
            src_ref=ys.at[pl.ds(peer * held, held)], dst_ref=yr.at[:, mine, :],
            send_sem=ex_send.at[2], recv_sem=ex_recv.at[2],
            device_id={"ctx": peer}, device_id_type=pl.DeviceIdType.MESH,
        )

    for d in near:
        back_copy(d).start()
    own_back = pltpu.make_async_copy(
        ys.at[pl.ds(me * held, held)], yr.at[:, mine, :], own_sem.at[2]
    )
    own_back.start()
    wait_bytes(wo, w_sem.at[3])
    own_back.wait()

    wait_bytes(yr.at[:, pl.ds(0, width - chans), :], ex_recv.at[2])

    for b in range(held):
        for c in range(0, width, 128):
            value = p1t[b, c : c + 128, :].astype(F32) * yr[b, c : c + 128, :].astype(F32)
            gated[b * block_len : (b + 1) * block_len, c : c + 128] = value.T.astype(BF16)

    def out_part(slot, h):
        return jnp.dot(gated[...], wo[slot, :, h * half : (h + 1) * half], preferred_element_type=F32)

    targets = {"a": over, "bu": up, "bd": dn, "c": None, "d": over, "eu": up, "ed": dn}
    places = {
        ("a", 0): 0, ("a", 1): 1, ("bu", 0): 2, ("bu", 1): 3, ("bd", 0): 4, ("bd", 1): 5,
        ("c", 0): 6, ("c", 1): 7, ("d", 0): 8, ("d", 1): 9, ("eu", 0): 10, ("eu", 1): 11,
        ("ed", 0): 12, ("ed", 1): 13,
    }

    def rs_copy(name, h):
        m = places[name, h]
        target = targets[name]
        if name == "c":
            target = up if h == 0 else dn
        return pltpu.make_async_remote_copy(
            src_ref=rout.at[m], dst_ref=rin.at[m], send_sem=rs_send.at[0], recv_sem=rs_recv.at[m],
            device_id=target, device_id_type=pl.DeviceIdType.MESH,
        )

    def send(name, h, value):
        rout[places[name, h]] = value.astype(BF16)
        rs_copy(name, h).start()

    def receive(name, h):
        rs_copy(name, h).wait_recv()
        return rin[places[name, h]].astype(F32)

    for name, slot, h in (
        ("a", 7, 0), ("bu", 6, 0), ("bd", 5, 1), ("a", 7, 1), ("bu", 6, 1), ("bd", 5, 0),
    ):
        send(name, h, out_part(slot, h))
    for slot in range(5):
        for h in range(2):
            part[slot * 2 + h] = out_part(slot, h)
    send("c", 0, part[8] + receive("a", 0))
    send("c", 1, part[9] + receive("a", 1))
    send("eu", 1, part[5])
    send("ed", 0, part[2])
    for h in range(2):
        send("d", h, part[6 + h] + receive("bu", h) + receive("bd", h))
    send("eu", 0, part[4] + receive("c", 0))
    send("ed", 1, part[3] + receive("c", 1))
    for h in range(2):
        total = part[h] + receive("d", h)
        total = total + receive("eu", h) + receive("ed", h)
        out_ref[:, h * half : (h + 1) * half] = total.astype(BF16)

    wait_bytes(tok.at[pl.ds(2, 14)], ag_send.at[0])
    wait_bytes(taps_t.at[pl.ds(0, width - chans), :], ex_send.at[0])
    wait_bytes(mx.at[pl.ds(0, blocks - held)], ex_send.at[1])
    wait_bytes(mx.at[pl.ds(0, blocks - held)], ex_send.at[2])
    wait_bytes(rout, rs_send.at[0])


def local(nctx, nch, block, tokens, filter_taps, block_order, in_weights, out_weights):
    rows, width = tokens.shape
    blocks = block_order.shape[0]
    block_len = rows * nctx // blocks
    half = width // 2
    chans = width // nctx
    held = rows // block_len
    long_blocks = rows * nctx // block
    forward, inverse = spectral_tables(block)
    dims = (nctx, nch, rows, width, block_len, block)
    hbm = pl.BlockSpec(memory_space=pl.ANY)
    dma = pltpu.SemaphoreType.DMA
    return pl.pallas_call(
        functools.partial(kernel, dims),
        out_shape=pltpu.VMEM((rows, width), BF16),
        in_specs=[hbm] * 7,
        out_specs=pl.BlockSpec(memory_space=pltpu.VMEM),
        scratch_shapes=[
            pltpu.VMEM((16, rows, half), BF16),
            pltpu.VMEM((8, 3, width, width), BF16),
            pltpu.VMEM((8, width, width), BF16),
            pltpu.VMEM((3, rows, width), F32),
            pltpu.VMEM(forward.shape, BF16),
            pltpu.VMEM(inverse.shape, BF16),
            pltpu.VMEM((rows, width), BF16),
            pltpu.VMEM((width, rows), BF16),
            pltpu.VMEM((long_blocks, chans, block), BF16),
            pltpu.VMEM((long_blocks, chans, block), F32),
            pltpu.VMEM((long_blocks, chans, block), F32),
            pltpu.VMEM((long_blocks, chans, block), F32),
            pltpu.VMEM((held, width, block_len), BF16),
            pltpu.VMEM((blocks, chans, block_len), BF16),
            pltpu.VMEM((long_blocks, chans, block), BF16),
            pltpu.VMEM((long_blocks, chans, 2 * block), F32),
            pltpu.VMEM((long_blocks, chans, 2 * block), F32),
            pltpu.VMEM((blocks, chans, block_len), BF16),
            pltpu.VMEM((blocks, chans, block_len), BF16),
            pltpu.VMEM((held, width, block_len), BF16),
            pltpu.VMEM((held, width, block_len), BF16),
            pltpu.VMEM((rows, width), BF16),
            pltpu.VMEM((10, rows, half), F32),
            pltpu.VMEM((14, rows, half), BF16),
            pltpu.VMEM((14, rows, half), BF16),
            pltpu.SMEM((blocks,), jnp.int32),
            pltpu.SMEM((blocks,), jnp.int32),
            dma((5,)), dma((4,)),
            dma((1,)), dma((28,)),
            dma((3,)), dma((3,)),
            dma((1,)), dma((14,)),
            dma((3,)),
        ],
        compiler_params=pltpu.CompilerParams(
            collective_id=0, has_side_effects=True, vmem_limit_bytes=56 * 2**20
        ),
        name="hyena_layer",
    )(block_order, tokens, filter_taps, in_weights, out_weights, jnp.asarray(forward), jnp.asarray(inverse))


def solution(mesh):
    placed = (P("ctx", "ch"), P("ctx", "ch"), P(), P(None, None, "ch"), P("ch", None))
    body = functools.partial(local, mesh.shape["ctx"], mesh.shape["ch"], 512)
    return jax.shard_map(body, mesh=mesh, in_specs=placed, out_specs=P("ctx", "ch"), check_vma=False)
```

```python
import functools
import math

import jax
import jax.numpy as jnp
import ml_dtypes
import numpy as np
from jax import lax
from jax.experimental import pallas as pl
from jax.experimental.pallas import tpu as pltpu
from jax.sharding import PartitionSpec as P

F32 = jnp.float32
BF16 = jnp.bfloat16


def spectral_tables(block):
    length = 2 * block
    index = np.arange(block)
    angles = 2.0 * math.pi * ((index[:, None] * index[None, :]) % length) / length
    real, imag = np.cos(angles), -np.sin(angles)
    imag[:, 0] = 1.0 - 2.0 * (index % 2)
    forward = np.concatenate([real, imag], 1).astype(ml_dtypes.bfloat16)
    later = index + block
    back = 2.0 * math.pi * ((index[:, None] * later[None, :]) % length) / length
    real, imag = 2.0 * np.cos(back) / length, -2.0 * np.sin(back) / length
    real[0] = 1.0 / length
    imag[0] = (1.0 - 2.0 * (later % 2)) / length
    inverse = np.concatenate([real, imag], 0).astype(ml_dtypes.bfloat16)
    return forward, inverse


ARRIVALS = (
    (1, 0), (2, 3), (1, 1), (2, 2), (3, 1), "p10", (3, 2), "p21", (1, 2), (2, 1), (3, 0), "p30", (1, 3), (2, 0),
    (3, 3), "p11", "p20", "p31", (4, 0), (4, 3), (4, 1), (4, 2), "p40", "p41", "filter",
    (5, 0), (5, 1), "p50", (6, 3), (6, 2), "p61", (5, 2), (5, 3), "p51", (6, 1), (6, 0), "p60",
    (7, 0), (7, 1), "p70", (7, 2), (7, 3), "p71",
)
FORWARDS = {
    (1, 0): ((4, 0), (5, 0)), (1, 1): ((4, 1),), (2, 3): ((4, 3), (6, 3)), (2, 2): ((4, 2),),
    (3, 0): ((6, 0),), (3, 1): ((5, 1), (6, 1)), (3, 2): ((5, 2), (6, 2)), (3, 3): ((5, 3),),
    (4, 0): ((7, 0),), (4, 1): ((7, 1),), (4, 2): ((7, 2),), (4, 3): ((7, 3),),
}


def kernel(
    dims, order_ref, tokens_ref, taps_ref, w_in_ref, w_out_ref, tab_f_ref, tab_i_ref, out_ref,
    tok, wv, wo, acc, tab_f, tab_i, taps_v, taps_t, ft, fr, fi, fz, mt, mx, xn, sp, tot, yn, ys, yr,
    p1t, gated, part, rin, rout, ord_ref, inv_ref,
    load_sem, w_sem, ag_send, ag_recv, ex_send, ex_recv, rs_send, rs_recv, own_sem,
):
    nctx, nch, rows, width, block_len, block = dims
    half = width // 2
    ny = nch // 2
    chans = width // nctx
    blocks = nctx * rows // block_len
    held = rows // block_len
    long_blocks = nctx * rows // block
    per_long = block // block_len
    near = sorted(range(1, nctx), key=lambda d: min(d, nctx - d))
    me = lax.axis_index("ctx")
    ch = lax.axis_index("ch")
    z = ch // ny
    y = ch % ny
    zo = 1 - z
    y_up = (y + 1) % ny
    y_dn = (y + ny - 1) % ny
    y_far = (y + 2) % ny
    up = {"ch": z * ny + y_up}
    dn = {"ch": z * ny + y_dn}
    over = {"ch": zo * ny + y}
    shard_of = (
        z * ny + y, z * ny + y_dn, z * ny + y_up, zo * ny + y,
        z * ny + y_far, zo * ny + y_dn, zo * ny + y_up, zo * ny + y_far,
    )

    def wait_bytes(ref, sem):
        pltpu.make_async_copy(ref, ref, sem).wait()

    barrier = pltpu.get_barrier_semaphore()
    for neighbour in (up, dn, over):
        pl.semaphore_signal(barrier, inc=1, device_id=neighbour, device_id_type=pl.DeviceIdType.MESH)
    for d in near[::-1]:
        pl.semaphore_signal(
            barrier, inc=1, device_id={"ctx": (me + d) % nctx}, device_id_type=pl.DeviceIdType.MESH
        )
    pl.semaphore_wait(barrier, 3 + nctx - 1)

    quarter = rows // 2

    def chunk(slot, c):
        return tok.at[slot * 2 + c // 2, pl.ds((c % 2) * quarter, quarter)]

    def message(slot, c, source, target):
        if source is None:
            source = tokens_ref.at[pl.ds((c % 2) * quarter, quarter), pl.ds((c // 2) * half, half)]
        else:
            source = chunk(source, c)
        return pltpu.make_async_remote_copy(
            src_ref=source, dst_ref=chunk(slot, c), send_sem=ag_send.at[0],
            recv_sem=ag_recv.at[(slot - 1) * 4 + c], device_id=target,
            device_id_type=pl.DeviceIdType.MESH,
        )

    gather = {}
    for c in range(4):
        gather[1, c] = message(1, c, None, up)
        gather[2, c] = message(2, c, None, dn)
        gather[3, c] = message(3, c, None, over)
        gather[4, c] = message(4, c, 1, up) if c < 2 else message(4, c, 2, dn)
        gather[5, c] = message(5, c, 1, over) if c == 0 else message(5, c, 3, up)
        gather[6, c] = message(6, c, 2, over) if c == 3 else message(6, c, 3, dn)
        gather[7, c] = message(7, c, 4, over)
    for keys in zip(((1, 0), (1, 1), (1, 2), (1, 3)), ((2, 3), (2, 2), (2, 1), (2, 0)), ((3, 1), (3, 2), (3, 0), (3, 3))):
        for key in keys:
            gather[key].start()

    taps_load = pltpu.make_async_copy(taps_ref, taps_v, load_sem.at[0])
    tab_f_load = pltpu.make_async_copy(tab_f_ref, tab_f, load_sem.at[1])
    tab_i_load = pltpu.make_async_copy(tab_i_ref, tab_i, load_sem.at[2])
    order_load = pltpu.make_async_copy(order_ref, ord_ref, load_sem.at[3])
    w_group = (0, 1, 1, 1, 2, 2, 2, 2)
    taps_load.start()
    for h in range(2):
        pltpu.make_async_copy(tokens_ref.at[:, pl.ds(h * half, half)], tok.at[h], load_sem.at[4]).start()
    for slot in range(8):
        start = pl.multiple_of(shard_of[slot] * width, width)
        pltpu.make_async_copy(
            w_in_ref.at[:, pl.ds(start, width), :], wv.at[slot], w_sem.at[w_group[slot]]
        ).start()
        if slot == 3:
            tab_f_load.start()
            order_load.start()
    tab_i_load.start()
    for slot in range(8):
        start = pl.multiple_of(shard_of[slot] * width, width)
        pltpu.make_async_copy(
            w_out_ref.at[:, pl.ds(start, width)], wo.at[slot], w_sem.at[3]
        ).start()

    taps_load.wait()
    for r in range(0, rows, 128):
        for c in range(0, width, 128):
            piece = taps_v[r : r + 128, c : c + 128].astype(F32)
            taps_t[c : c + 128, r : r + 128] = piece.T.astype(BF16)

    per_rows = block // rows
    mine = pl.ds(pl.multiple_of(me * chans, chans), chans)
    my_lags = pl.ds(pl.multiple_of((me % per_rows) * rows, rows), rows)

    def channels_of(peer):
        return pl.ds(pl.multiple_of(peer * chans, chans), chans)

    def taps_copy(d):
        peer = (me + d) % nctx
        return pltpu.make_async_remote_copy(
            src_ref=taps_t.at[channels_of(peer), :], dst_ref=ft.at[me // per_rows, :, my_lags],
            send_sem=ex_send.at[0], recv_sem=ex_recv.at[0],
            device_id={"ctx": peer}, device_id_type=pl.DeviceIdType.MESH,
        )

    def start_taps(d, c):
        taps_copy(d).start()
        return c

    lax.fori_loop(1, nctx, start_taps, 0)
    own_taps = pltpu.make_async_copy(
        taps_t.at[mine, :], ft.at[me // per_rows, :, my_lags], own_sem.at[0]
    )
    own_taps.start()

    def invert(j, c):
        found = jnp.int32(0)
        for s in range(blocks):
            found = jnp.where(ord_ref[s] == j, jnp.int32(s), found)
        inv_ref[j] = found
        return c

    def project(slot, h, streams, first=False):
        left = tok[slot * 2 + h]
        for k in streams:
            value = jnp.dot(left, wv[slot, k, h * half : (h + 1) * half, :], preferred_element_type=F32)
            if first:
                acc[k] = value
            else:
                acc[k] += value

    def filter_spectra():
        own_taps.wait()
        wait_bytes(taps_t.at[pl.ds(0, width - chans), :], ex_recv.at[0])
        tab_f_load.wait()
        lane = lax.broadcasted_iota(jnp.int32, (chans, block), 1)
        sign = jnp.where(lane % 2 == 0, 1.0, -1.0).astype(F32)
        before_r = jnp.zeros((chans, block), F32)
        before_i = jnp.zeros((chans, block), F32)
        for j in range(long_blocks):
            spectrum = jnp.dot(ft[j], tab_f[...], preferred_element_type=F32)
            now_r, now_i = spectrum[:, :block], spectrum[:, block:]
            real = before_r + sign * now_r
            imag = before_i + sign * now_i
            fr[j] = real
            fi[j] = jnp.where(lane == 0, 0.0, imag)
            fz[j] = jnp.where(lane == 0, imag, real)
            before_r, before_i = now_r, now_i
        order_load.wait()
        lax.fori_loop(0, blocks, invert, 0)

    wait_bytes(tok.at[pl.ds(0, 2)], load_sem.at[4])
    wait_bytes(wv.at[pl.ds(0, 1)], w_sem.at[0])
    project(0, 0, (0, 1, 2), first=True)
    waited = 0
    for step in ("p01",) + ARRIVALS:
        if step == "filter":
            filter_spectra()
        elif isinstance(step, str):
            slot, h = int(step[1]), int(step[2])
            if w_group[slot] > waited:
                waited = w_group[slot]
                wait_bytes(wv.at[pl.ds(1, 3)] if waited == 1 else wv.at[pl.ds(4, 4)], w_sem.at[waited])
            project(slot, h, (0, 2) if step == ARRIVALS[-1] else (0, 1, 2))
        else:
            gather[step].wait_recv()
            for key in FORWARDS.get(step, ()):
                gather[key].start()

    for c in range(0, width, 128):
        for b in range(held):
            at = slice(b * block_len, (b + 1) * block_len)
            first = acc[0, at, c : c + 128].astype(BF16).astype(F32)
            third = acc[2, at, c : c + 128].astype(BF16).astype(F32)
            mt[b, c : c + 128, :] = (first * third).T.astype(BF16)

    def mixed_copy(d):
        peer = (me + d) % nctx
        return pltpu.make_async_remote_copy(
            src_ref=mt.at[:, channels_of(peer), :], dst_ref=mx.at[pl.ds(me * held, held)],
            send_sem=ex_send.at[1], recv_sem=ex_recv.at[1],
            device_id={"ctx": peer}, device_id_type=pl.DeviceIdType.MESH,
        )

    for d in near:
        mixed_copy(d).start()
    own_mixed = pltpu.make_async_copy(
        mt.at[:, mine, :], mx.at[pl.ds(me * held, held)], own_sem.at[1]
    )
    own_mixed.start()

    project(7, 1, (1,))
    for c in range(0, width, 128):
        for b in range(held):
            at = slice(b * block_len, (b + 1) * block_len)
            p1t[b, c : c + 128, :] = acc[1, at, c : c + 128].T.astype(BF16)
    tab_i_load.wait()

    own_mixed.wait()

    wait_bytes(mx.at[pl.ds(0, blocks - held)], ex_recv.at[1])

    for j in range(blocks):
        at = (j % per_long) * block_len
        xn[j // per_long, :, at : at + block_len] = mx[inv_ref[j]]
    count = long_blocks * chans
    spectra = jnp.dot(xn[...].reshape(count, block), tab_f[...], preferred_element_type=F32)
    sp[...] = spectra.reshape(long_blocks, chans, 2 * block)

    lane_tiles = block // 128

    def products(tile, c):
        r0 = pl.multiple_of((tile // lane_tiles) * 8, 8)
        f0 = pl.multiple_of((tile % lane_tiles) * 128, 128)
        at = (pl.ds(r0, 8), pl.ds(f0, 128))
        at_i = (pl.ds(r0, 8), pl.ds(block + f0, 128))
        data_r = [sp[(j,) + at] for j in range(long_blocks)]
        data_i = [sp[(j,) + at_i] for j in range(long_blocks)]
        filt_r = [fr[(j,) + at] for j in range(long_blocks)]
        filt_i = [fi[(j,) + at] for j in range(long_blocks)]
        filt_z = [fz[(j,) + at] for j in range(long_blocks)]
        for i in range(long_blocks):
            total_r = data_r[0] * filt_r[i] - data_i[0] * filt_i[i]
            total_i = data_r[0] * filt_i[i] + data_i[0] * filt_z[i]
            for j in range(1, i + 1):
                total_r = total_r + (data_r[j] * filt_r[i - j] - data_i[j] * filt_i[i - j])
                total_i = total_i + (data_r[j] * filt_i[i - j] + data_i[j] * filt_z[i - j])
            tot[(i,) + at] = total_r
            tot[(i,) + at_i] = total_i
        return c

    lax.fori_loop(0, (chans // 8) * lane_tiles, products, 0)
    result = jnp.dot(
        tot[...].reshape(count, 2 * block).astype(BF16), tab_i[...], preferred_element_type=F32
    ).astype(BF16)
    for j in range(blocks):
        at = (j % per_long) * block_len
        r0 = (j // per_long) * chans
        yn[j] = result[r0 : r0 + chans, at : at + block_len]
    for s in range(blocks):
        ys[s] = yn[ord_ref[s]]

    def back_copy(d):
        peer = (me + d) % nctx
        return pltpu.make_async_remote_copy(
            src_ref=ys.at[pl.ds(peer * held, held)], dst_ref=yr.at[:, mine, :],
            send_sem=ex_send.at[2], recv_sem=ex_recv.at[2],
            device_id={"ctx": peer}, device_id_type=pl.DeviceIdType.MESH,
        )

    for d in near:
        back_copy(d).start()
    own_back = pltpu.make_async_copy(
        ys.at[pl.ds(me * held, held)], yr.at[:, mine, :], own_sem.at[2]
    )
    own_back.start()
    wait_bytes(wo, w_sem.at[3])
    own_back.wait()

    wait_bytes(yr.at[:, pl.ds(0, width - chans), :], ex_recv.at[2])

    for b in range(held):
        for c in range(0, width, 128):
            value = p1t[b, c : c + 128, :].astype(F32) * yr[b, c : c + 128, :].astype(F32)
            gated[b * block_len : (b + 1) * block_len, c : c + 128] = value.T.astype(BF16)

    targets = {"a": over, "bu": up, "bd": dn, "d": over, "eu": up, "ed": dn}
    names = ("a", "bu", "bd", "c", "d", "eu", "ed")

    def rs_copy(name, c):
        m = names.index(name) * 4 + c
        target = targets[name] if name != "c" else up if c < 2 else dn
        return pltpu.make_async_remote_copy(
            src_ref=rout.at[m], dst_ref=rin.at[m], send_sem=rs_send.at[0], recv_sem=rs_recv.at[m],
            device_id=target, device_id_type=pl.DeviceIdType.MESH,
        )

    def send(name, c, value):
        rout[names.index(name) * 4 + c] = value.astype(BF16)
        rs_copy(name, c).start()

    def receive(name, c):
        rs_copy(name, c).wait_recv()
        return rin[names.index(name) * 4 + c].astype(F32)

    def out_part(slot, h):
        return jnp.dot(gated[...], wo[slot, :, h * half : (h + 1) * half], preferred_element_type=F32)

    def share(slot, c):
        return part[slot * 2 + c // 2, (c % 2) * quarter : (c % 2 + 1) * quarter, :]

    for name, slot, h, order in (
        ("bu", 6, 0, (0, 1)), ("bd", 5, 1, (1, 0)), ("a", 7, 0, (0, 1)), ("a", 7, 1, (1, 0)),
        ("bu", 6, 1, (0, 1)), ("bd", 5, 0, (1, 0)),
    ):
        value = out_part(slot, h)
        for r in order:
            send(name, h * 2 + r, value[r * quarter : (r + 1) * quarter])
    for slot in (4, 3, 2, 1, 0):
        for h in range(2):
            part[slot * 2 + h] = out_part(slot, h)
    send("c", 0, share(4, 0) + receive("a", 0))
    send("c", 3, share(4, 3) + receive("a", 3))
    send("ed", 1, share(1, 1))
    send("c", 1, share(4, 1) + receive("a", 1))
    send("eu", 2, share(2, 2))
    send("d", 1, share(3, 1) + receive("bu", 1) + receive("bd", 1))
    send("d", 2, share(3, 2) + receive("bu", 2) + receive("bd", 2))
    send("c", 2, share(4, 2) + receive("a", 2))
    send("ed", 0, share(1, 0))
    send("eu", 3, share(2, 3))
    send("d", 0, share(3, 0) + receive("bu", 0) + receive("bd", 0))
    send("d", 3, share(3, 3) + receive("bu", 3) + receive("bd", 3))
    send("eu", 0, share(2, 0) + receive("c", 0))
    send("ed", 3, share(1, 3) + receive("c", 3))
    send("eu", 1, share(2, 1) + receive("c", 1))
    send("ed", 2, share(1, 2) + receive("c", 2))
    for c in (0, 3, 1, 2):
        total = share(0, c) + receive("d", c)
        total = total + receive("eu", c) + receive("ed", c)
        at_r, at_c = (c % 2) * quarter, (c // 2) * half
        out_ref[at_r : at_r + quarter, at_c : at_c + half] = total.astype(BF16)

    wait_bytes(tok.at[pl.ds(2, 14)], ag_send.at[0])
    wait_bytes(taps_t.at[pl.ds(0, width - chans), :], ex_send.at[0])
    wait_bytes(mx.at[pl.ds(0, blocks - held)], ex_send.at[1])
    wait_bytes(mx.at[pl.ds(0, blocks - held)], ex_send.at[2])
    wait_bytes(rout, rs_send.at[0])


def local(nctx, nch, block, tokens, filter_taps, block_order, in_weights, out_weights):
    rows, width = tokens.shape
    blocks = block_order.shape[0]
    block_len = rows * nctx // blocks
    half = width // 2
    chans = width // nctx
    held = rows // block_len
    long_blocks = rows * nctx // block
    forward, inverse = spectral_tables(block)
    dims = (nctx, nch, rows, width, block_len, block)
    hbm = pl.BlockSpec(memory_space=pl.ANY)
    dma = pltpu.SemaphoreType.DMA
    return pl.pallas_call(
        functools.partial(kernel, dims),
        out_shape=pltpu.VMEM((rows, width), BF16),
        in_specs=[hbm] * 7,
        out_specs=pl.BlockSpec(memory_space=pltpu.VMEM),
        scratch_shapes=[
            pltpu.VMEM((16, rows, half), BF16),
            pltpu.VMEM((8, 3, width, width), BF16),
            pltpu.VMEM((8, width, width), BF16),
            pltpu.VMEM((3, rows, width), F32),
            pltpu.VMEM(forward.shape, BF16),
            pltpu.VMEM(inverse.shape, BF16),
            pltpu.VMEM((rows, width), BF16),
            pltpu.VMEM((width, rows), BF16),
            pltpu.VMEM((long_blocks, chans, block), BF16),
            pltpu.VMEM((long_blocks, chans, block), F32),
            pltpu.VMEM((long_blocks, chans, block), F32),
            pltpu.VMEM((long_blocks, chans, block), F32),
            pltpu.VMEM((held, width, block_len), BF16),
            pltpu.VMEM((blocks, chans, block_len), BF16),
            pltpu.VMEM((long_blocks, chans, block), BF16),
            pltpu.VMEM((long_blocks, chans, 2 * block), F32),
            pltpu.VMEM((long_blocks, chans, 2 * block), F32),
            pltpu.VMEM((blocks, chans, block_len), BF16),
            pltpu.VMEM((blocks, chans, block_len), BF16),
            pltpu.VMEM((held, width, block_len), BF16),
            pltpu.VMEM((held, width, block_len), BF16),
            pltpu.VMEM((rows, width), BF16),
            pltpu.VMEM((10, rows, half), F32),
            pltpu.VMEM((28, rows // 2, half), BF16),
            pltpu.VMEM((28, rows // 2, half), BF16),
            pltpu.SMEM((blocks,), jnp.int32),
            pltpu.SMEM((blocks,), jnp.int32),
            dma((5,)), dma((4,)),
            dma((1,)), dma((28,)),
            dma((3,)), dma((3,)),
            dma((1,)), dma((28,)),
            dma((3,)),
        ],
        compiler_params=pltpu.CompilerParams(
            collective_id=0, has_side_effects=True, vmem_limit_bytes=56 * 2**20
        ),
        name="hyena_layer",
    )(block_order, tokens, filter_taps, in_weights, out_weights, jnp.asarray(forward), jnp.asarray(inverse))


def solution(mesh):
    placed = (P("ctx", "ch"), P("ctx", "ch"), P(), P(None, None, "ch"), P("ch", None))
    body = functools.partial(local, mesh.shape["ctx"], mesh.shape["ch"], 512)
    return jax.shard_map(body, mesh=mesh, in_specs=placed, out_specs=P("ctx", "ch"), check_vma=False)
```

```python
import functools
import math

import jax
import jax.numpy as jnp
import ml_dtypes
import numpy as np
from jax import lax
from jax.experimental import pallas as pl
from jax.experimental.pallas import tpu as pltpu
from jax.sharding import PartitionSpec as P

F32 = jnp.float32
BF16 = jnp.bfloat16


def spectral_tables(block):
    length = 2 * block
    index = np.arange(block)
    angles = 2.0 * math.pi * ((index[:, None] * index[None, :]) % length) / length
    real, imag = np.cos(angles), -np.sin(angles)
    imag[:, 0] = 1.0 - 2.0 * (index % 2)
    forward = np.concatenate([real, imag], 1).astype(ml_dtypes.bfloat16)
    later = index + block
    back = 2.0 * math.pi * ((index[:, None] * later[None, :]) % length) / length
    real, imag = 2.0 * np.cos(back) / length, -2.0 * np.sin(back) / length
    real[0] = 1.0 / length
    imag[0] = (1.0 - 2.0 * (later % 2)) / length
    inverse = np.concatenate([real, imag], 0).astype(ml_dtypes.bfloat16)
    return forward, inverse


ARRIVALS = (
    (1, 0), (2, 3), (1, 1), (2, 2), (3, 1), "p10", (3, 2), "p21", (1, 2), (2, 1), (3, 0), "p30", (1, 3), (2, 0),
    (3, 3), "p11", "p20", "p31", (4, 0), (4, 3), (4, 1), (4, 2), "p40", "p41",
    (5, 0), (5, 1), "p50", (6, 3), (6, 2), "p61", (5, 2), (5, 3), "p51", (6, 1), (6, 0), "p60",
    (7, 0), (7, 1), "p70", (7, 2), (7, 3), "p71",
)
FORWARDS = {
    (1, 0): ((4, 0), (5, 0)), (1, 1): ((4, 1),), (2, 3): ((4, 3),), (2, 2): ((4, 2),),
    (3, 0): ((6, 0),), (3, 1): ((5, 1), (6, 1)), (3, 2): ((5, 2), (6, 2)), (3, 3): ((5, 3), (6, 3)),
    (4, 0): ((7, 0),), (4, 1): ((7, 1),), (4, 2): ((7, 2),), (4, 3): ((7, 3),),
}


def kernel(
    dims, order_ref, tokens_ref, taps_ref, w_in_ref, w_out_ref, tab_f_ref, tab_i_ref, out_ref,
    tok, wv, wo, acc, tab_f, tab_i, taps_v, taps_t, ft, fr, fi, fz, mt, mx, xn, sp, tot, yn, ys, yr,
    p1t, gated, part, rin, rout, ord_ref, inv_ref,
    load_sem, w_sem, ag_send, ag_recv, ex_send, ex_recv, rs_send, rs_recv, own_sem,
):
    nctx, nch, rows, width, block_len, block = dims
    half = width // 2
    ny = nch // 2
    chans = width // nctx
    blocks = nctx * rows // block_len
    held = rows // block_len
    long_blocks = nctx * rows // block
    per_long = block // block_len
    near = sorted(range(1, nctx), key=lambda d: min(d, nctx - d))
    me = lax.axis_index("ctx")
    ch = lax.axis_index("ch")
    z = ch // ny
    y = ch % ny
    zo = 1 - z
    y_up = (y + 1) % ny
    y_dn = (y + ny - 1) % ny
    y_far = (y + 2) % ny
    up = {"ch": z * ny + y_up}
    dn = {"ch": z * ny + y_dn}
    over = {"ch": zo * ny + y}
    shard_of = (
        z * ny + y, z * ny + y_dn, z * ny + y_up, zo * ny + y,
        z * ny + y_far, zo * ny + y_dn, zo * ny + y_up, zo * ny + y_far,
    )

    def wait_bytes(ref, sem):
        pltpu.make_async_copy(ref, ref, sem).wait()

    barrier = pltpu.get_barrier_semaphore()
    for neighbour in (up, dn, over):
        pl.semaphore_signal(barrier, inc=1, device_id=neighbour, device_id_type=pl.DeviceIdType.MESH)
    for d in near[::-1]:
        pl.semaphore_signal(
            barrier, inc=1, device_id={"ctx": (me + d) % nctx}, device_id_type=pl.DeviceIdType.MESH
        )
    pl.semaphore_wait(barrier, 3 + nctx - 1)

    quarter = rows // 2

    def chunk(slot, c):
        return tok.at[slot * 2 + c // 2, pl.ds((c % 2) * quarter, quarter)]

    def message(slot, c, source, target):
        if source is None:
            source = tokens_ref.at[pl.ds((c % 2) * quarter, quarter), pl.ds((c // 2) * half, half)]
        else:
            source = chunk(source, c)
        return pltpu.make_async_remote_copy(
            src_ref=source, dst_ref=chunk(slot, c), send_sem=ag_send.at[0],
            recv_sem=ag_recv.at[(slot - 1) * 4 + c], device_id=target,
            device_id_type=pl.DeviceIdType.MESH,
        )

    gather = {}
    for c in range(4):
        gather[1, c] = message(1, c, None, up)
        gather[2, c] = message(2, c, None, dn)
        gather[3, c] = message(3, c, None, over)
        gather[4, c] = message(4, c, 1, up) if c < 2 else message(4, c, 2, dn)
        gather[5, c] = message(5, c, 1, over) if c == 0 else message(5, c, 3, up)
        gather[6, c] = message(6, c, 3, dn)
        gather[7, c] = message(7, c, 4, over)
    for keys in zip(((1, 0), (1, 1), (1, 2), (1, 3)), ((2, 3), (2, 2), (2, 1), (2, 0)), ((3, 1), (3, 2), (3, 0), (3, 3))):
        for key in keys:
            gather[key].start()

    taps_load = pltpu.make_async_copy(taps_ref, taps_v, load_sem.at[0])
    tab_f_load = pltpu.make_async_copy(tab_f_ref, tab_f, load_sem.at[1])
    tab_i_load = pltpu.make_async_copy(tab_i_ref, tab_i, load_sem.at[2])
    order_load = pltpu.make_async_copy(order_ref, ord_ref, load_sem.at[3])
    w_group = (0, 1, 1, 1, 2, 2, 2, 2)
    taps_load.start()
    for h in range(2):
        pltpu.make_async_copy(tokens_ref.at[:, pl.ds(h * half, half)], tok.at[h], load_sem.at[4]).start()
    for slot in range(8):
        start = pl.multiple_of(shard_of[slot] * width, width)
        pltpu.make_async_copy(
            w_in_ref.at[:, pl.ds(start, width), :], wv.at[slot], w_sem.at[w_group[slot]]
        ).start()
        if slot == 3:
            tab_f_load.start()
            order_load.start()
    tab_i_load.start()
    for slot in range(8):
        start = pl.multiple_of(shard_of[slot] * width, width)
        pltpu.make_async_copy(
            w_out_ref.at[:, pl.ds(start, width)], wo.at[slot], w_sem.at[3]
        ).start()

    taps_load.wait()
    for r in range(0, rows, 128):
        for c in range(0, width, 128):
            piece = taps_v[r : r + 128, c : c + 128].astype(F32)
            taps_t[c : c + 128, r : r + 128] = piece.T.astype(BF16)

    per_rows = block // rows
    mine = pl.ds(pl.multiple_of(me * chans, chans), chans)
    my_lags = pl.ds(pl.multiple_of((me % per_rows) * rows, rows), rows)

    def channels_of(peer):
        return pl.ds(pl.multiple_of(peer * chans, chans), chans)

    def taps_copy(d):
        peer = (me + d) % nctx
        return pltpu.make_async_remote_copy(
            src_ref=taps_t.at[channels_of(peer), :], dst_ref=ft.at[me // per_rows, :, my_lags],
            send_sem=ex_send.at[0], recv_sem=ex_recv.at[0],
            device_id={"ctx": peer}, device_id_type=pl.DeviceIdType.MESH,
        )

    def start_taps(d, c):
        taps_copy(d).start()
        return c

    lax.fori_loop(1, nctx, start_taps, 0)
    own_taps = pltpu.make_async_copy(
        taps_t.at[mine, :], ft.at[me // per_rows, :, my_lags], own_sem.at[0]
    )
    own_taps.start()

    def invert(j, c):
        found = jnp.int32(0)
        for s in range(blocks):
            found = jnp.where(ord_ref[s] == j, jnp.int32(s), found)
        inv_ref[j] = found
        return c

    def project(slot, h, streams, first=False):
        left = tok[slot * 2 + h]
        for k in streams:
            value = jnp.dot(left, wv[slot, k, h * half : (h + 1) * half, :], preferred_element_type=F32)
            if first:
                acc[k] = value
            else:
                acc[k] += value

    def filter_spectra():
        own_taps.wait()
        wait_bytes(taps_t.at[pl.ds(0, width - chans), :], ex_recv.at[0])
        tab_f_load.wait()
        lane = lax.broadcasted_iota(jnp.int32, (chans, block), 1)
        sign = jnp.where(lane % 2 == 0, 1.0, -1.0).astype(F32)
        before_r = jnp.zeros((chans, block), F32)
        before_i = jnp.zeros((chans, block), F32)
        for j in range(long_blocks):
            spectrum = jnp.dot(ft[j], tab_f[...], preferred_element_type=F32)
            now_r, now_i = spectrum[:, :block], spectrum[:, block:]
            real = before_r + sign * now_r
            imag = before_i + sign * now_i
            fr[j] = real
            fi[j] = jnp.where(lane == 0, 0.0, imag)
            fz[j] = jnp.where(lane == 0, imag, real)
            before_r, before_i = now_r, now_i
        order_load.wait()
        lax.fori_loop(0, blocks, invert, 0)

    wait_bytes(tok.at[pl.ds(0, 2)], load_sem.at[4])
    wait_bytes(wv.at[pl.ds(0, 1)], w_sem.at[0])
    project(0, 0, (0, 1, 2), first=True)
    waited = 0
    for step in ("p01",) + ARRIVALS:
        if step == "taps":
            lax.fori_loop(1, nctx, start_taps, 0)
        elif isinstance(step, str):
            slot, h = int(step[1]), int(step[2])
            if w_group[slot] > waited:
                waited = w_group[slot]
                wait_bytes(wv.at[pl.ds(1, 3)] if waited == 1 else wv.at[pl.ds(4, 4)], w_sem.at[waited])
            project(slot, h, (0, 2) if step == ARRIVALS[-1] else (0, 1, 2))
        else:
            gather[step].wait_recv()
            for key in FORWARDS.get(step, ()):
                gather[key].start()

    def mixed_copy(peer):
        return pltpu.make_async_remote_copy(
            src_ref=mt.at[:, channels_of(peer), :], dst_ref=mx.at[pl.ds(me * held, held)],
            send_sem=ex_send.at[1], recv_sem=ex_recv.at[1],
            device_id={"ctx": peer}, device_id_type=pl.DeviceIdType.MESH,
        )

    groups = width // 128
    members = nctx // groups
    for turn in sorted(range(groups), key=lambda k: -min(k, groups - k)):
        group = (me // members + turn) % groups
        c = pl.ds(pl.multiple_of(group * 128, 128), 128)
        for b in range(held):
            at = slice(b * block_len, (b + 1) * block_len)
            first = acc[0, at, c].astype(BF16).astype(F32)
            third = acc[2, at, c].astype(BF16).astype(F32)
            mt[b, c, :] = (first * third).T.astype(BF16)
        for k in range(1 if turn == 0 else 0, members):
            mixed_copy(group * members + (me + k) % members).start()
    own_mixed = pltpu.make_async_copy(
        mt.at[:, mine, :], mx.at[pl.ds(me * held, held)], own_sem.at[1]
    )
    own_mixed.start()

    project(7, 1, (1,))
    for c in range(0, width, 128):
        for b in range(held):
            at = slice(b * block_len, (b + 1) * block_len)
            p1t[b, c : c + 128, :] = acc[1, at, c : c + 128].T.astype(BF16)
    filter_spectra()
    tab_i_load.wait()

    own_mixed.wait()

    wait_bytes(mx.at[pl.ds(0, blocks - held)], ex_recv.at[1])

    for j in range(blocks):
        at = (j % per_long) * block_len
        xn[j // per_long, :, at : at + block_len] = mx[inv_ref[j]]
    count = long_blocks * chans
    spectra = jnp.dot(xn[...].reshape(count, block), tab_f[...], preferred_element_type=F32)
    sp[...] = spectra.reshape(long_blocks, chans, 2 * block)

    lane_tiles = block // 128

    def products(tile, c):
        r0 = pl.multiple_of((tile // lane_tiles) * 8, 8)
        f0 = pl.multiple_of((tile % lane_tiles) * 128, 128)
        at = (pl.ds(r0, 8), pl.ds(f0, 128))
        at_i = (pl.ds(r0, 8), pl.ds(block + f0, 128))
        data_r = [sp[(j,) + at] for j in range(long_blocks)]
        data_i = [sp[(j,) + at_i] for j in range(long_blocks)]
        filt_r = [fr[(j,) + at] for j in range(long_blocks)]
        filt_i = [fi[(j,) + at] for j in range(long_blocks)]
        filt_z = [fz[(j,) + at] for j in range(long_blocks)]
        for i in range(long_blocks):
            total_r = data_r[0] * filt_r[i] - data_i[0] * filt_i[i]
            total_i = data_r[0] * filt_i[i] + data_i[0] * filt_z[i]
            for j in range(1, i + 1):
                total_r = total_r + (data_r[j] * filt_r[i - j] - data_i[j] * filt_i[i - j])
                total_i = total_i + (data_r[j] * filt_i[i - j] + data_i[j] * filt_z[i - j])
            tot[(i,) + at] = total_r
            tot[(i,) + at_i] = total_i
        return c

    lax.fori_loop(0, (chans // 8) * lane_tiles, products, 0)
    result = jnp.dot(
        tot[...].reshape(count, 2 * block).astype(BF16), tab_i[...], preferred_element_type=F32
    ).astype(BF16)
    for j in range(blocks):
        at = (j % per_long) * block_len
        r0 = (j // per_long) * chans
        yn[j] = result[r0 : r0 + chans, at : at + block_len]
    def back_copy(peer):
        return pltpu.make_async_remote_copy(
            src_ref=ys.at[pl.ds(peer * held, held)], dst_ref=yr.at[:, mine, :],
            send_sem=ex_send.at[2], recv_sem=ex_recv.at[2],
            device_id={"ctx": peer}, device_id_type=pl.DeviceIdType.MESH,
        )

    for d in near[::-1] + [0]:
        peer = (me + d) % nctx
        for b in range(held):
            ys[peer * held + b] = yn[ord_ref[peer * held + b]]
        if d > 0:
            back_copy(peer).start()
    own_back = pltpu.make_async_copy(
        ys.at[pl.ds(me * held, held)], yr.at[:, mine, :], own_sem.at[2]
    )
    own_back.start()
    wait_bytes(wo, w_sem.at[3])
    own_back.wait()

    wait_bytes(yr.at[:, pl.ds(0, width - chans), :], ex_recv.at[2])

    for b in range(held):
        for c in range(0, width, 128):
            value = p1t[b, c : c + 128, :].astype(F32) * yr[b, c : c + 128, :].astype(F32)
            gated[b * block_len : (b + 1) * block_len, c : c + 128] = value.T.astype(BF16)

    targets = {"a": over, "bz": over, "bu": up, "bd": dn, "d": over, "eu": up, "ed": dn}
    names = ("a", "bu", "bd", "c", "d", "eu", "ed", "bz")

    def place(name, c):
        return {("bz", 0): 4, ("bz", 3): 11}.get((name, c), names.index(name) * 4 + c)

    def rs_copy(name, c):
        m = place(name, c)
        target = targets[name] if name != "c" else up if c < 2 else dn
        return pltpu.make_async_remote_copy(
            src_ref=rout.at[m], dst_ref=rin.at[m], send_sem=rs_send.at[0], recv_sem=rs_recv.at[m],
            device_id=target, device_id_type=pl.DeviceIdType.MESH,
        )

    def send(name, c, value):
        rout[place(name, c)] = value.astype(BF16)
        rs_copy(name, c).start()

    def receive(name, c):
        rs_copy(name, c).wait_recv()
        return rin[place(name, c)].astype(F32)

    def out_part(slot, h):
        return jnp.dot(gated[...], wo[slot, :, h * half : (h + 1) * half], preferred_element_type=F32)

    def share(slot, c):
        return part[slot * 2 + c // 2, (c % 2) * quarter : (c % 2 + 1) * quarter, :]

    half_0, half_3 = out_part(6, 0), out_part(5, 1)
    send("bu", 1, half_0[quarter:])
    send("bd", 2, half_3[:quarter])
    for name, slot, h, order in (("a", 7, 0, (0, 1)), ("a", 7, 1, (1, 0)), ("bu", 6, 1, (0, 1)), ("bd", 5, 0, (1, 0))):
        value = out_part(slot, h)
        for r in order:
            send(name, h * 2 + r, value[r * quarter : (r + 1) * quarter])
    send("bz", 0, half_0[:quarter])
    send("bz", 3, half_3[quarter:])
    for slot in (4, 3, 2, 1, 0):
        for h in range(2):
            part[slot * 2 + h] = out_part(slot, h)
    send("c", 0, share(4, 0) + receive("a", 0))
    send("c", 3, share(4, 3) + receive("a", 3))
    send("ed", 1, share(1, 1))
    send("c", 1, share(4, 1) + receive("a", 1))
    send("eu", 2, share(2, 2))
    send("d", 1, share(3, 1) + receive("bu", 1) + receive("bd", 1))
    send("d", 2, share(3, 2) + receive("bu", 2) + receive("bd", 2))
    send("c", 2, share(4, 2) + receive("a", 2))
    send("ed", 0, share(1, 0))
    send("eu", 3, share(2, 3))
    send("d", 0, share(3, 0) + receive("bd", 0))
    send("d", 3, share(3, 3) + receive("bu", 3))
    send("eu", 0, share(2, 0) + receive("c", 0) + receive("bz", 0))
    send("ed", 3, share(1, 3) + receive("c", 3) + receive("bz", 3))
    send("eu", 1, share(2, 1) + receive("c", 1))
    send("ed", 2, share(1, 2) + receive("c", 2))
    for c in (0, 3, 1, 2):
        total = share(0, c) + receive("d", c)
        total = total + receive("eu", c) + receive("ed", c)
        at_r, at_c = (c % 2) * quarter, (c // 2) * half
        out_ref[at_r : at_r + quarter, at_c : at_c + half] = total.astype(BF16)

    wait_bytes(tok.at[pl.ds(2, 14)], ag_send.at[0])
    wait_bytes(taps_t.at[pl.ds(0, width - chans), :], ex_send.at[0])
    wait_bytes(mx.at[pl.ds(0, blocks - held)], ex_send.at[1])
    wait_bytes(mx.at[pl.ds(0, blocks - held)], ex_send.at[2])
    wait_bytes(rout, rs_send.at[0])


def local(nctx, nch, block, tokens, filter_taps, block_order, in_weights, out_weights):
    rows, width = tokens.shape
    blocks = block_order.shape[0]
    block_len = rows * nctx // blocks
    half = width // 2
    chans = width // nctx
    held = rows // block_len
    long_blocks = rows * nctx // block
    forward, inverse = spectral_tables(block)
    dims = (nctx, nch, rows, width, block_len, block)
    hbm = pl.BlockSpec(memory_space=pl.ANY)
    dma = pltpu.SemaphoreType.DMA
    return pl.pallas_call(
        functools.partial(kernel, dims),
        out_shape=pltpu.VMEM((rows, width), BF16),
        in_specs=[hbm] * 7,
        out_specs=pl.BlockSpec(memory_space=pltpu.VMEM),
        scratch_shapes=[
            pltpu.VMEM((16, rows, half), BF16),
            pltpu.VMEM((8, 3, width, width), BF16),
            pltpu.VMEM((8, width, width), BF16),
            pltpu.VMEM((3, rows, width), F32),
            pltpu.VMEM(forward.shape, BF16),
            pltpu.VMEM(inverse.shape, BF16),
            pltpu.VMEM((rows, width), BF16),
            pltpu.VMEM((width, rows), BF16),
            pltpu.VMEM((long_blocks, chans, block), BF16),
            pltpu.VMEM((long_blocks, chans, block), F32),
            pltpu.VMEM((long_blocks, chans, block), F32),
            pltpu.VMEM((long_blocks, chans, block), F32),
            pltpu.VMEM((held, width, block_len), BF16),
            pltpu.VMEM((blocks, chans, block_len), BF16),
            pltpu.VMEM((long_blocks, chans, block), BF16),
            pltpu.VMEM((long_blocks, chans, 2 * block), F32),
            pltpu.VMEM((long_blocks, chans, 2 * block), F32),
            pltpu.VMEM((blocks, chans, block_len), BF16),
            pltpu.VMEM((blocks, chans, block_len), BF16),
            pltpu.VMEM((held, width, block_len), BF16),
            pltpu.VMEM((held, width, block_len), BF16),
            pltpu.VMEM((rows, width), BF16),
            pltpu.VMEM((10, rows, half), F32),
            pltpu.VMEM((28, rows // 2, half), BF16),
            pltpu.VMEM((28, rows // 2, half), BF16),
            pltpu.SMEM((blocks,), jnp.int32),
            pltpu.SMEM((blocks,), jnp.int32),
            dma((5,)), dma((4,)),
            dma((1,)), dma((28,)),
            dma((3,)), dma((3,)),
            dma((1,)), dma((28,)),
            dma((3,)),
        ],
        compiler_params=pltpu.CompilerParams(
            collective_id=0, has_side_effects=True, vmem_limit_bytes=56 * 2**20
        ),
        name="hyena_layer",
    )(block_order, tokens, filter_taps, in_weights, out_weights, jnp.asarray(forward), jnp.asarray(inverse))


def solution(mesh):
    placed = (P("ctx", "ch"), P("ctx", "ch"), P(), P(None, None, "ch"), P("ch", None))
    body = functools.partial(local, mesh.shape["ctx"], mesh.shape["ch"], 512)
    return jax.shard_map(body, mesh=mesh, in_specs=placed, out_specs=P("ctx", "ch"), check_vma=False)
```

```python
import functools
import math

import jax
import jax.numpy as jnp
import ml_dtypes
import numpy as np
from jax import lax
from jax.experimental import pallas as pl
from jax.experimental.pallas import tpu as pltpu
from jax.sharding import PartitionSpec as P

F32 = jnp.float32
BF16 = jnp.bfloat16


def spectral_tables(block):
    length = 2 * block
    index = np.arange(block)
    angles = 2.0 * math.pi * ((index[:, None] * index[None, :]) % length) / length
    real, imag = np.cos(angles), -np.sin(angles)
    imag[:, 0] = 1.0 - 2.0 * (index % 2)
    forward = np.concatenate([real, imag], 1).astype(ml_dtypes.bfloat16)
    later = index + block
    back = 2.0 * math.pi * ((index[:, None] * later[None, :]) % length) / length
    real, imag = 2.0 * np.cos(back) / length, -2.0 * np.sin(back) / length
    real[0] = 1.0 / length
    imag[0] = (1.0 - 2.0 * (later % 2)) / length
    inverse = np.concatenate([real, imag], 0).astype(ml_dtypes.bfloat16)
    return forward, inverse


ARRIVALS = (
    (1, 0), (2, 3), (1, 1), (2, 2), (3, 1), "p10", (3, 2), "p21", (1, 2), (2, 1), (3, 0), "p30", (1, 3), (2, 0),
    (3, 3), "p11", "p20", "p31", (4, 0), (4, 3), (4, 1), (4, 2), "p40", "p41", "invert",
    (5, 0), (5, 1), "p50", (6, 3), (6, 2), "p61", (5, 2), (5, 3), "p51", (6, 1), (6, 0), "p60",
    (7, 0), (7, 1), "p70", (7, 2), (7, 3), "p71",
)
FORWARDS = {
    (1, 0): ((4, 0), (5, 0)), (1, 1): ((4, 1),), (2, 3): ((4, 3),), (2, 2): ((4, 2),),
    (3, 0): ((6, 0),), (3, 1): ((5, 1), (6, 1)), (3, 2): ((5, 2), (6, 2)), (3, 3): ((5, 3), (6, 3)),
    (4, 0): ((7, 0),), (4, 1): ((7, 1),), (4, 2): ((7, 2),), (4, 3): ((7, 3),),
}


def kernel(
    dims, order_ref, tokens_ref, taps_ref, w_in_ref, w_out_ref, tab_f_ref, tab_i_ref, out_ref,
    tok, wv, wo, acc, tab_f, tab_i, taps_v, taps_t, ft, fr, fi, fz, mt, mx, xn, sp, tot, yn, ys, yr,
    p1t, gated, part, rin, rout, ord_ref, inv_ref,
    load_sem, w_sem, ag_send, ag_recv, ex_send, ex_recv, rs_send, rs_recv, own_sem,
):
    nctx, nch, rows, width, block_len, block = dims
    half = width // 2
    ny = nch // 2
    chans = width // nctx
    blocks = nctx * rows // block_len
    held = rows // block_len
    long_blocks = nctx * rows // block
    per_long = block // block_len
    near = sorted(range(1, nctx), key=lambda d: min(d, nctx - d))
    me = lax.axis_index("ctx")
    ch = lax.axis_index("ch")
    z = ch // ny
    y = ch % ny
    zo = 1 - z
    y_up = (y + 1) % ny
    y_dn = (y + ny - 1) % ny
    y_far = (y + 2) % ny
    up = {"ch": z * ny + y_up}
    dn = {"ch": z * ny + y_dn}
    over = {"ch": zo * ny + y}
    shard_of = (
        z * ny + y, z * ny + y_dn, z * ny + y_up, zo * ny + y,
        z * ny + y_far, zo * ny + y_dn, zo * ny + y_up, zo * ny + y_far,
    )

    def wait_bytes(ref, sem):
        pltpu.make_async_copy(ref, ref, sem).wait()

    barrier = pltpu.get_barrier_semaphore()
    for neighbour in (up, dn, over):
        pl.semaphore_signal(barrier, inc=1, device_id=neighbour, device_id_type=pl.DeviceIdType.MESH)
    for d in near[::-1]:
        pl.semaphore_signal(
            barrier, inc=1, device_id={"ctx": (me + d) % nctx}, device_id_type=pl.DeviceIdType.MESH
        )
    pl.semaphore_wait(barrier, 3 + nctx - 1)

    quarter = rows // 2

    def chunk(slot, c):
        return tok.at[slot * 2 + c // 2, pl.ds((c % 2) * quarter, quarter)]

    def message(slot, c, source, target):
        if source is None:
            source = tokens_ref.at[pl.ds((c % 2) * quarter, quarter), pl.ds((c // 2) * half, half)]
        else:
            source = chunk(source, c)
        return pltpu.make_async_remote_copy(
            src_ref=source, dst_ref=chunk(slot, c), send_sem=ag_send.at[0],
            recv_sem=ag_recv.at[(slot - 1) * 4 + c], device_id=target,
            device_id_type=pl.DeviceIdType.MESH,
        )

    gather = {}
    for c in range(4):
        gather[1, c] = message(1, c, None, up)
        gather[2, c] = message(2, c, None, dn)
        gather[3, c] = message(3, c, None, over)
        gather[4, c] = message(4, c, 1, up) if c < 2 else message(4, c, 2, dn)
        gather[5, c] = message(5, c, 1, over) if c == 0 else message(5, c, 3, up)
        gather[6, c] = message(6, c, 3, dn)
        gather[7, c] = message(7, c, 4, over)
    for keys in zip(((1, 0), (1, 1), (1, 2), (1, 3)), ((2, 3), (2, 2), (2, 1), (2, 0)), ((3, 1), (3, 2), (3, 0), (3, 3))):
        for key in keys:
            gather[key].start()

    taps_load = pltpu.make_async_copy(taps_ref, taps_v, load_sem.at[0])
    tab_f_load = pltpu.make_async_copy(tab_f_ref, tab_f, load_sem.at[1])
    tab_i_load = pltpu.make_async_copy(tab_i_ref, tab_i, load_sem.at[2])
    order_load = pltpu.make_async_copy(order_ref, ord_ref, load_sem.at[3])
    w_group = (0, 1, 1, 1, 2, 2, 2, 2)
    taps_load.start()
    for h in range(2):
        pltpu.make_async_copy(tokens_ref.at[:, pl.ds(h * half, half)], tok.at[h], load_sem.at[4]).start()
    for slot in range(8):
        start = pl.multiple_of(shard_of[slot] * width, width)
        pltpu.make_async_copy(
            w_in_ref.at[:, pl.ds(start, width), :], wv.at[slot], w_sem.at[w_group[slot]]
        ).start()
        if slot == 3:
            tab_f_load.start()
            order_load.start()
    tab_i_load.start()
    for slot in range(8):
        start = pl.multiple_of(shard_of[slot] * width, width)
        pltpu.make_async_copy(
            w_out_ref.at[:, pl.ds(start, width)], wo.at[slot], w_sem.at[3]
        ).start()

    taps_load.wait()
    for r in range(0, rows, 128):
        for c in range(0, width, 128):
            piece = taps_v[r : r + 128, c : c + 128].astype(F32)
            taps_t[c : c + 128, r : r + 128] = piece.T.astype(BF16)

    per_rows = block // rows
    mine = pl.ds(pl.multiple_of(me * chans, chans), chans)
    my_lags = pl.ds(pl.multiple_of((me % per_rows) * rows, rows), rows)

    def channels_of(peer):
        return pl.ds(pl.multiple_of(peer * chans, chans), chans)

    def taps_copy(d):
        peer = (me + d) % nctx
        return pltpu.make_async_remote_copy(
            src_ref=taps_t.at[channels_of(peer), :], dst_ref=ft.at[me // per_rows, :, my_lags],
            send_sem=ex_send.at[0], recv_sem=ex_recv.at[0],
            device_id={"ctx": peer}, device_id_type=pl.DeviceIdType.MESH,
        )

    def start_taps(d, c):
        taps_copy(d).start()
        return c

    lax.fori_loop(1, nctx, start_taps, 0)
    own_taps = pltpu.make_async_copy(
        taps_t.at[mine, :], ft.at[me // per_rows, :, my_lags], own_sem.at[0]
    )
    own_taps.start()

    def invert(j, c):
        found = jnp.int32(0)
        for s in range(blocks):
            found = jnp.where(ord_ref[s] == j, jnp.int32(s), found)
        inv_ref[j] = found
        return c

    def project(slot, h, streams, first=False):
        left = tok[slot * 2 + h]
        for k in streams:
            value = jnp.dot(left, wv[slot, k, h * half : (h + 1) * half, :], preferred_element_type=F32)
            if first:
                acc[k] = value
            else:
                acc[k] += value

    def filter_spectra():
        own_taps.wait()
        wait_bytes(taps_t.at[pl.ds(0, width - chans), :], ex_recv.at[0])
        tab_f_load.wait()
        lane = lax.broadcasted_iota(jnp.int32, (chans, block), 1)
        sign = jnp.where(lane % 2 == 0, 1.0, -1.0).astype(F32)
        count = long_blocks * chans
        spectra = jnp.dot(ft[...].reshape(count, block), tab_f[...], preferred_element_type=F32)
        sp[...] = spectra.reshape(long_blocks, chans, 2 * block)
        before_r = jnp.zeros((chans, block), F32)
        before_i = jnp.zeros((chans, block), F32)
        for j in range(long_blocks):
            now_r, now_i = sp[j, :, :block], sp[j, :, block:]
            real = before_r + sign * now_r
            imag = before_i + sign * now_i
            fr[j] = real
            fi[j] = jnp.where(lane == 0, 0.0, imag)
            fz[j] = jnp.where(lane == 0, imag, real)
            before_r, before_i = now_r, now_i

    wait_bytes(tok.at[pl.ds(0, 2)], load_sem.at[4])
    wait_bytes(wv.at[pl.ds(0, 1)], w_sem.at[0])
    project(0, 0, (0, 1, 2), first=True)
    waited = 0
    for step in ("p01",) + ARRIVALS:
        if step == "invert":
            order_load.wait()
            lax.fori_loop(0, blocks, invert, 0)
        elif isinstance(step, str):
            slot, h = int(step[1]), int(step[2])
            if w_group[slot] > waited:
                waited = w_group[slot]
                wait_bytes(wv.at[pl.ds(1, 3)] if waited == 1 else wv.at[pl.ds(4, 4)], w_sem.at[waited])
            project(slot, h, (0, 2) if step == ARRIVALS[-1] else (0, 1, 2))
        else:
            gather[step].wait_recv()
            for key in FORWARDS.get(step, ()):
                gather[key].start()

    def mixed_copy(peer):
        return pltpu.make_async_remote_copy(
            src_ref=mt.at[:, channels_of(peer), :], dst_ref=mx.at[pl.ds(me * held, held)],
            send_sem=ex_send.at[1], recv_sem=ex_recv.at[1],
            device_id={"ctx": peer}, device_id_type=pl.DeviceIdType.MESH,
        )

    groups = width // 128
    members = nctx // groups
    for turn in sorted(range(groups), key=lambda k: -min(k, groups - k)):
        group = (me // members + turn) % groups
        c = pl.ds(pl.multiple_of(group * 128, 128), 128)
        for b in range(held):
            at = slice(b * block_len, (b + 1) * block_len)
            first = acc[0, at, c].astype(BF16).astype(F32)
            third = acc[2, at, c].astype(BF16).astype(F32)
            mt[b, c, :] = (first * third).T.astype(BF16)
        for k in range(1 if turn == 0 else 0, members):
            mixed_copy(group * members + (me + k) % members).start()
    own_mixed = pltpu.make_async_copy(
        mt.at[:, mine, :], mx.at[pl.ds(me * held, held)], own_sem.at[1]
    )
    own_mixed.start()

    project(7, 1, (1,))
    for c in range(0, width, 128):
        for b in range(held):
            at = slice(b * block_len, (b + 1) * block_len)
            p1t[b, c : c + 128, :] = acc[1, at, c : c + 128].T.astype(BF16)
    filter_spectra()
    tab_i_load.wait()

    own_mixed.wait()

    wait_bytes(mx.at[pl.ds(0, blocks - held)], ex_recv.at[1])

    for j in range(blocks):
        at = (j % per_long) * block_len
        xn[j // per_long, :, at : at + block_len] = mx[inv_ref[j]]
    count = long_blocks * chans
    spectra = jnp.dot(xn[...].reshape(count, block), tab_f[...], preferred_element_type=F32)
    sp[...] = spectra.reshape(long_blocks, chans, 2 * block)

    lane_tiles = block // 128

    def products(tile, c):
        r0 = pl.multiple_of((tile // lane_tiles) * 8, 8)
        f0 = pl.multiple_of((tile % lane_tiles) * 128, 128)
        at = (pl.ds(r0, 8), pl.ds(f0, 128))
        at_i = (pl.ds(r0, 8), pl.ds(block + f0, 128))
        data_r = [sp[(j,) + at] for j in range(long_blocks)]
        data_i = [sp[(j,) + at_i] for j in range(long_blocks)]
        filt_r = [fr[(j,) + at] for j in range(long_blocks)]
        filt_i = [fi[(j,) + at] for j in range(long_blocks)]
        filt_z = [fz[(j,) + at] for j in range(long_blocks)]
        for i in range(long_blocks):
            total_r = data_r[0] * filt_r[i] - data_i[0] * filt_i[i]
            total_i = data_r[0] * filt_i[i] + data_i[0] * filt_z[i]
            for j in range(1, i + 1):
                total_r = total_r + (data_r[j] * filt_r[i - j] - data_i[j] * filt_i[i - j])
                total_i = total_i + (data_r[j] * filt_i[i - j] + data_i[j] * filt_z[i - j])
            tot[(i,) + at] = total_r
            tot[(i,) + at_i] = total_i
        return c

    lax.fori_loop(0, (chans // 8) * lane_tiles, products, 0, unroll=True)
    result = jnp.dot(
        tot[...].reshape(count, 2 * block).astype(BF16), tab_i[...], preferred_element_type=F32
    ).astype(BF16)
    for j in range(blocks):
        at = (j % per_long) * block_len
        r0 = (j // per_long) * chans
        yn[j] = result[r0 : r0 + chans, at : at + block_len]
    def back_copy(peer):
        return pltpu.make_async_remote_copy(
            src_ref=ys.at[pl.ds(peer * held, held)], dst_ref=yr.at[:, mine, :],
            send_sem=ex_send.at[2], recv_sem=ex_recv.at[2],
            device_id={"ctx": peer}, device_id_type=pl.DeviceIdType.MESH,
        )

    for d in near[::-1] + [0]:
        peer = (me + d) % nctx
        for b in range(held):
            ys[peer * held + b] = yn[ord_ref[peer * held + b]]
        if d > 0:
            back_copy(peer).start()
    own_back = pltpu.make_async_copy(
        ys.at[pl.ds(me * held, held)], yr.at[:, mine, :], own_sem.at[2]
    )
    own_back.start()
    wait_bytes(wo, w_sem.at[3])
    own_back.wait()

    wait_bytes(yr.at[:, pl.ds(0, width - chans), :], ex_recv.at[2])

    for b in range(held):
        for c in range(0, width, 128):
            value = p1t[b, c : c + 128, :].astype(F32) * yr[b, c : c + 128, :].astype(F32)
            gated[b * block_len : (b + 1) * block_len, c : c + 128] = value.T.astype(BF16)

    targets = {"a": over, "bz": over, "bu": up, "bd": dn, "d": over, "eu": up, "ed": dn}
    names = ("a", "bu", "bd", "c", "d", "eu", "ed", "bz")

    def place(name, c):
        return {("bz", 0): 4, ("bz", 3): 11}.get((name, c), names.index(name) * 4 + c)

    def rs_copy(name, c):
        m = place(name, c)
        target = targets[name] if name != "c" else up if c < 2 else dn
        return pltpu.make_async_remote_copy(
            src_ref=rout.at[m], dst_ref=rin.at[m], send_sem=rs_send.at[0], recv_sem=rs_recv.at[m],
            device_id=target, device_id_type=pl.DeviceIdType.MESH,
        )

    def send(name, c, value):
        rout[place(name, c)] = value.astype(BF16)
        rs_copy(name, c).start()

    def receive(name, c):
        rs_copy(name, c).wait_recv()
        return rin[place(name, c)].astype(F32)

    def out_part(slot, h):
        return jnp.dot(gated[...], wo[slot, :, h * half : (h + 1) * half], preferred_element_type=F32)

    def share(slot, c):
        return part[slot * 2 + c // 2, (c % 2) * quarter : (c % 2 + 1) * quarter, :]

    half_0, half_3 = out_part(6, 0), out_part(5, 1)
    send("bu", 1, half_0[quarter:])
    send("bd", 2, half_3[:quarter])
    for name, slot, h, order in (("a", 7, 0, (0, 1)), ("a", 7, 1, (1, 0)), ("bu", 6, 1, (0, 1)), ("bd", 5, 0, (1, 0))):
        value = out_part(slot, h)
        for r in order:
            send(name, h * 2 + r, value[r * quarter : (r + 1) * quarter])
    send("bz", 0, half_0[:quarter])
    send("bz", 3, half_3[quarter:])
    for slot in (4, 3, 2, 1, 0):
        for h in range(2):
            part[slot * 2 + h] = out_part(slot, h)
    send("c", 0, share(4, 0) + receive("a", 0))
    send("c", 3, share(4, 3) + receive("a", 3))
    send("ed", 1, share(1, 1))
    send("c", 1, share(4, 1) + receive("a", 1))
    send("eu", 2, share(2, 2))
    send("d", 1, share(3, 1) + receive("bu", 1) + receive("bd", 1))
    send("d", 2, share(3, 2) + receive("bu", 2) + receive("bd", 2))
    send("c", 2, share(4, 2) + receive("a", 2))
    send("ed", 0, share(1, 0))
    send("eu", 3, share(2, 3))
    send("d", 0, share(3, 0) + receive("bd", 0))
    send("d", 3, share(3, 3) + receive("bu", 3))
    send("eu", 0, share(2, 0) + receive("c", 0) + receive("bz", 0))
    send("ed", 3, share(1, 3) + receive("c", 3) + receive("bz", 3))
    send("eu", 1, share(2, 1) + receive("c", 1))
    send("ed", 2, share(1, 2) + receive("c", 2))
    for c in (0, 3, 1, 2):
        total = share(0, c) + receive("d", c)
        total = total + receive("eu", c) + receive("ed", c)
        at_r, at_c = (c % 2) * quarter, (c // 2) * half
        out_ref[at_r : at_r + quarter, at_c : at_c + half] = total.astype(BF16)

    wait_bytes(tok.at[pl.ds(2, 14)], ag_send.at[0])
    wait_bytes(taps_t.at[pl.ds(0, width - chans), :], ex_send.at[0])
    wait_bytes(mx.at[pl.ds(0, blocks - held)], ex_send.at[1])
    wait_bytes(mx.at[pl.ds(0, blocks - held)], ex_send.at[2])
    wait_bytes(rout, rs_send.at[0])


def local(nctx, nch, block, tokens, filter_taps, block_order, in_weights, out_weights):
    rows, width = tokens.shape
    blocks = block_order.shape[0]
    block_len = rows * nctx // blocks
    half = width // 2
    chans = width // nctx
    held = rows // block_len
    long_blocks = rows * nctx // block
    forward, inverse = spectral_tables(block)
    dims = (nctx, nch, rows, width, block_len, block)
    hbm = pl.BlockSpec(memory_space=pl.ANY)
    dma = pltpu.SemaphoreType.DMA
    return pl.pallas_call(
        functools.partial(kernel, dims),
        out_shape=pltpu.VMEM((rows, width), BF16),
        in_specs=[hbm] * 7,
        out_specs=pl.BlockSpec(memory_space=pltpu.VMEM),
        scratch_shapes=[
            pltpu.VMEM((16, rows, half), BF16),
            pltpu.VMEM((8, 3, width, width), BF16),
            pltpu.VMEM((8, width, width), BF16),
            pltpu.VMEM((3, rows, width), F32),
            pltpu.VMEM(forward.shape, BF16),
            pltpu.VMEM(inverse.shape, BF16),
            pltpu.VMEM((rows, width), BF16),
            pltpu.VMEM((width, rows), BF16),
            pltpu.VMEM((long_blocks, chans, block), BF16),
            pltpu.VMEM((long_blocks, chans, block), F32),
            pltpu.VMEM((long_blocks, chans, block), F32),
            pltpu.VMEM((long_blocks, chans, block), F32),
            pltpu.VMEM((held, width, block_len), BF16),
            pltpu.VMEM((blocks, chans, block_len), BF16),
            pltpu.VMEM((long_blocks, chans, block), BF16),
            pltpu.VMEM((long_blocks, chans, 2 * block), F32),
            pltpu.VMEM((long_blocks, chans, 2 * block), F32),
            pltpu.VMEM((blocks, chans, block_len), BF16),
            pltpu.VMEM((blocks, chans, block_len), BF16),
            pltpu.VMEM((held, width, block_len), BF16),
            pltpu.VMEM((held, width, block_len), BF16),
            pltpu.VMEM((rows, width), BF16),
            pltpu.VMEM((10, rows, half), F32),
            pltpu.VMEM((28, rows // 2, half), BF16),
            pltpu.VMEM((28, rows // 2, half), BF16),
            pltpu.SMEM((blocks,), jnp.int32),
            pltpu.SMEM((blocks,), jnp.int32),
            dma((5,)), dma((4,)),
            dma((1,)), dma((28,)),
            dma((3,)), dma((3,)),
            dma((1,)), dma((28,)),
            dma((3,)),
        ],
        compiler_params=pltpu.CompilerParams(
            collective_id=0, has_side_effects=True, vmem_limit_bytes=56 * 2**20
        ),
        name="hyena_layer",
    )(block_order, tokens, filter_taps, in_weights, out_weights, jnp.asarray(forward), jnp.asarray(inverse))


def solution(mesh):
    placed = (P("ctx", "ch"), P("ctx", "ch"), P(), P(None, None, "ch"), P("ch", None))
    body = functools.partial(local, mesh.shape["ctx"], mesh.shape["ch"], 512)
    return jax.shard_map(body, mesh=mesh, in_specs=placed, out_specs=P("ctx", "ch"), check_vma=False)
```

```python
import functools
import math

import jax
import jax.numpy as jnp
import ml_dtypes
import numpy as np
from jax import lax
from jax.experimental import pallas as pl
from jax.experimental.pallas import tpu as pltpu
from jax.sharding import PartitionSpec as P

F32 = jnp.float32
BF16 = jnp.bfloat16


def spectral_tables(block):
    length = 2 * block
    index = np.arange(block)
    angles = 2.0 * math.pi * ((index[:, None] * index[None, :]) % length) / length
    real, imag = np.cos(angles), -np.sin(angles)
    imag[:, 0] = 1.0 - 2.0 * (index % 2)
    forward = np.concatenate([real, imag], 1).astype(ml_dtypes.bfloat16)
    later = index + block
    back = 2.0 * math.pi * ((index[:, None] * later[None, :]) % length) / length
    real, imag = 2.0 * np.cos(back) / length, -2.0 * np.sin(back) / length
    real[0] = 1.0 / length
    imag[0] = (1.0 - 2.0 * (later % 2)) / length
    inverse = np.concatenate([real, imag], 0).astype(ml_dtypes.bfloat16)
    return forward, inverse


ARRIVALS = (
    (1, 0), (2, 3), (1, 1), (2, 2), (3, 1), "p10", (3, 2), "p21", (1, 2), (2, 1), (3, 0), "p30", (1, 3), (2, 0),
    (3, 3), "p11", "p20", "p31", (4, 0), (4, 3), (4, 1), (4, 2), "p40", "p41", "invert",
    (5, 0), (5, 1), "p50", (6, 3), (6, 2), "p61", (5, 2), (5, 3), "p51", (6, 1), (6, 0), "p60",
    (7, 0), (7, 1), "p70", (7, 2), (7, 3), "p71",
)
FORWARDS = {
    (1, 0): ((4, 0), (5, 0)), (1, 1): ((4, 1),), (2, 3): ((4, 3),), (2, 2): ((4, 2),),
    (3, 0): ((6, 0),), (3, 1): ((5, 1), (6, 1)), (3, 2): ((5, 2), (6, 2)), (3, 3): ((5, 3), (6, 3)),
    (4, 0): ((7, 0),), (4, 1): ((7, 1),), (4, 2): ((7, 2),), (4, 3): ((7, 3),),
}


def kernel(
    dims, order_ref, tokens_ref, taps_ref, w_in_ref, w_out_ref, tab_f_ref, tab_i_ref, out_ref,
    tok, wv, wo, acc, tab_f, tab_i, taps_v, taps_t, ft, fr, fi, fz, mt, mx, xn, sp, tot, yn, ys, yr,
    p1t, gated, part, rin, rout, ord_ref, inv_ref,
    load_sem, w_sem, ag_send, ag_recv, ex_send, ex_recv, rs_send, rs_recv, own_sem,
):
    nctx, nch, rows, width, block_len, block = dims
    half = width // 2
    ny = nch // 2
    chans = width // nctx
    blocks = nctx * rows // block_len
    held = rows // block_len
    long_blocks = nctx * rows // block
    per_long = block // block_len
    near = sorted(range(1, nctx), key=lambda d: min(d, nctx - d))
    me = lax.axis_index("ctx")
    ch = lax.axis_index("ch")
    z = ch // ny
    y = ch % ny
    zo = 1 - z
    y_up = (y + 1) % ny
    y_dn = (y + ny - 1) % ny
    y_far = (y + 2) % ny
    up = {"ch": z * ny + y_up}
    dn = {"ch": z * ny + y_dn}
    over = {"ch": zo * ny + y}
    shard_of = (
        z * ny + y, z * ny + y_dn, z * ny + y_up, zo * ny + y,
        z * ny + y_far, zo * ny + y_dn, zo * ny + y_up, zo * ny + y_far,
    )

    def wait_bytes(ref, sem):
        pltpu.make_async_copy(ref, ref, sem).wait()

    barrier = pltpu.get_barrier_semaphore()
    for neighbour in (up, dn, over):
        pl.semaphore_signal(barrier, inc=1, device_id=neighbour, device_id_type=pl.DeviceIdType.MESH)
    for d in near[::-1]:
        pl.semaphore_signal(
            barrier, inc=1, device_id={"ctx": (me + d) % nctx}, device_id_type=pl.DeviceIdType.MESH
        )
    pl.semaphore_wait(barrier, 3 + nctx - 1)

    quarter = rows // 2

    def chunk(slot, c):
        return tok.at[slot * 2 + c // 2, pl.ds((c % 2) * quarter, quarter)]

    def message(slot, c, source, target):
        if source is None:
            source = tokens_ref.at[pl.ds((c % 2) * quarter, quarter), pl.ds((c // 2) * half, half)]
        else:
            source = chunk(source, c)
        return pltpu.make_async_remote_copy(
            src_ref=source, dst_ref=chunk(slot, c), send_sem=ag_send.at[0],
            recv_sem=ag_recv.at[(slot - 1) * 4 + c], device_id=target,
            device_id_type=pl.DeviceIdType.MESH,
        )

    gather = {}
    for c in range(4):
        gather[1, c] = message(1, c, None, up)
        gather[2, c] = message(2, c, None, dn)
        gather[3, c] = message(3, c, None, over)
        gather[4, c] = message(4, c, 1, up) if c < 2 else message(4, c, 2, dn)
        gather[5, c] = message(5, c, 1, over) if c == 0 else message(5, c, 3, up)
        gather[6, c] = message(6, c, 3, dn)
        gather[7, c] = message(7, c, 4, over)
    for keys in zip(((1, 0), (1, 1), (1, 2), (1, 3)), ((2, 3), (2, 2), (2, 1), (2, 0)), ((3, 1), (3, 2), (3, 0), (3, 3))):
        for key in keys:
            gather[key].start()

    taps_load = pltpu.make_async_copy(taps_ref, taps_v, load_sem.at[0])
    tab_f_load = pltpu.make_async_copy(tab_f_ref, tab_f, load_sem.at[1])
    tab_i_load = pltpu.make_async_copy(tab_i_ref, tab_i, load_sem.at[2])
    order_load = pltpu.make_async_copy(order_ref, ord_ref, load_sem.at[3])
    w_group = (0, 1, 1, 1, 2, 2, 2, 2)
    taps_load.start()
    for h in range(2):
        pltpu.make_async_copy(tokens_ref.at[:, pl.ds(h * half, half)], tok.at[h], load_sem.at[4]).start()
    for slot in range(8):
        start = pl.multiple_of(shard_of[slot] * width, width)
        pltpu.make_async_copy(
            w_in_ref.at[:, pl.ds(start, width), :], wv.at[slot], w_sem.at[w_group[slot]]
        ).start()
        if slot == 3:
            tab_f_load.start()
            order_load.start()
    tab_i_load.start()
    for slot in range(8):
        start = pl.multiple_of(shard_of[slot] * width, width)
        pltpu.make_async_copy(
            w_out_ref.at[:, pl.ds(start, width)], wo.at[slot], w_sem.at[3]
        ).start()

    taps_load.wait()
    for r in range(0, rows, 128):
        for c in range(0, width, 128):
            piece = taps_v[r : r + 128, c : c + 128].astype(F32)
            taps_t[c : c + 128, r : r + 128] = piece.T.astype(BF16)

    per_rows = block // rows
    mine = pl.ds(pl.multiple_of(me * chans, chans), chans)
    my_lags = pl.ds(pl.multiple_of((me % per_rows) * rows, rows), rows)

    def channels_of(peer):
        return pl.ds(pl.multiple_of(peer * chans, chans), chans)

    def taps_copy(d):
        peer = (me + d) % nctx
        return pltpu.make_async_remote_copy(
            src_ref=taps_t.at[channels_of(peer), :], dst_ref=ft.at[me // per_rows, :, my_lags],
            send_sem=ex_send.at[0], recv_sem=ex_recv.at[0],
            device_id={"ctx": peer}, device_id_type=pl.DeviceIdType.MESH,
        )

    def start_taps(d, c):
        taps_copy(d).start()
        return c

    lax.fori_loop(1, nctx, start_taps, 0)
    own_taps = pltpu.make_async_copy(
        taps_t.at[mine, :], ft.at[me // per_rows, :, my_lags], own_sem.at[0]
    )
    own_taps.start()

    def invert(j, c):
        found = jnp.int32(0)
        for s in range(blocks):
            found = jnp.where(ord_ref[s] == j, jnp.int32(s), found)
        inv_ref[j] = found
        return c

    def project(slot, h, streams, first=False):
        left = tok[slot * 2 + h]
        for k in streams:
            value = jnp.dot(left, wv[slot, k, h * half : (h + 1) * half, :], preferred_element_type=F32)
            if first:
                acc[k] = value
            else:
                acc[k] += value

    def filter_spectra():
        own_taps.wait()
        wait_bytes(taps_t.at[pl.ds(0, width - chans), :], ex_recv.at[0])
        tab_f_load.wait()
        lane = lax.broadcasted_iota(jnp.int32, (chans, block), 1)
        sign = jnp.where(lane % 2 == 0, 1.0, -1.0).astype(F32)
        count = long_blocks * chans
        spectra = jnp.dot(ft[...].reshape(count, block), tab_f[...], preferred_element_type=F32)
        sp[...] = spectra.reshape(long_blocks, chans, 2 * block)
        before_r = jnp.zeros((chans, block), F32)
        before_i = jnp.zeros((chans, block), F32)
        for j in range(long_blocks):
            now_r, now_i = sp[j, :, :block], sp[j, :, block:]
            real = before_r + sign * now_r
            imag = before_i + sign * now_i
            fr[j] = real
            fi[j] = jnp.where(lane == 0, 0.0, imag)
            fz[j] = jnp.where(lane == 0, imag, real)
            before_r, before_i = now_r, now_i

    wait_bytes(tok.at[pl.ds(0, 2)], load_sem.at[4])
    wait_bytes(wv.at[pl.ds(0, 1)], w_sem.at[0])
    project(0, 0, (0, 1, 2), first=True)
    waited = 0
    for step in ("p01",) + ARRIVALS:
        if step == "invert":
            order_load.wait()
            lax.fori_loop(0, blocks, invert, 0)
        elif isinstance(step, str):
            slot, h = int(step[1]), int(step[2])
            if w_group[slot] > waited:
                waited = w_group[slot]
                wait_bytes(wv.at[pl.ds(1, 3)] if waited == 1 else wv.at[pl.ds(4, 4)], w_sem.at[waited])
            project(slot, h, (0, 2) if step == ARRIVALS[-1] else (0, 1, 2))
        else:
            gather[step].wait_recv()
            for key in FORWARDS.get(step, ()):
                gather[key].start()

    def mixed_copy(peer):
        return pltpu.make_async_remote_copy(
            src_ref=mt.at[:, channels_of(peer), :], dst_ref=mx.at[pl.ds(me * held, held)],
            send_sem=ex_send.at[1], recv_sem=ex_recv.at[1],
            device_id={"ctx": peer}, device_id_type=pl.DeviceIdType.MESH,
        )

    groups = width // 128
    members = nctx // groups
    for turn in sorted(range(groups), key=lambda k: -min(k, groups - k)):
        group = (me // members + turn) % groups
        c = pl.ds(pl.multiple_of(group * 128, 128), 128)
        for b in range(held):
            at = slice(b * block_len, (b + 1) * block_len)
            first = acc[0, at, c].astype(BF16).astype(F32)
            third = acc[2, at, c].astype(BF16).astype(F32)
            mt[b, c, :] = (first * third).T.astype(BF16)
        for k in range(1 if turn == 0 else 0, members):
            mixed_copy(group * members + (me + k) % members).start()
    own_mixed = pltpu.make_async_copy(
        mt.at[:, mine, :], mx.at[pl.ds(me * held, held)], own_sem.at[1]
    )
    own_mixed.start()

    project(7, 1, (1,))
    for c in range(0, width, 128):
        for b in range(held):
            at = slice(b * block_len, (b + 1) * block_len)
            p1t[b, c : c + 128, :] = acc[1, at, c : c + 128].T.astype(BF16)
    filter_spectra()
    tab_i_load.wait()

    own_mixed.wait()

    wait_bytes(mx.at[pl.ds(0, blocks - held)], ex_recv.at[1])

    for j in range(blocks):
        at = (j % per_long) * block_len
        xn[j // per_long, :, at : at + block_len] = mx[inv_ref[j]]
    count = long_blocks * chans
    spectra = jnp.dot(xn[...].reshape(count, block), tab_f[...], preferred_element_type=F32)
    sp[...] = spectra.reshape(long_blocks, chans, 2 * block)

    lane_tiles = block // 128

    def products(tile, c):
        r0 = pl.multiple_of((tile // lane_tiles) * 8, 8)
        f0 = pl.multiple_of((tile % lane_tiles) * 128, 128)
        at = (pl.ds(r0, 8), pl.ds(f0, 128))
        at_i = (pl.ds(r0, 8), pl.ds(block + f0, 128))
        data_r = [sp[(j,) + at] for j in range(long_blocks)]
        data_i = [sp[(j,) + at_i] for j in range(long_blocks)]
        filt_r = [fr[(j,) + at] for j in range(long_blocks)]
        filt_i = [fi[(j,) + at] for j in range(long_blocks)]
        filt_z = [fz[(j,) + at] for j in range(long_blocks)]
        for i in range(long_blocks):
            total_r = data_r[0] * filt_r[i] - data_i[0] * filt_i[i]
            total_i = data_r[0] * filt_i[i] + data_i[0] * filt_z[i]
            for j in range(1, i + 1):
                total_r = total_r + (data_r[j] * filt_r[i - j] - data_i[j] * filt_i[i - j])
                total_i = total_i + (data_r[j] * filt_i[i - j] + data_i[j] * filt_z[i - j])
            tot[(i,) + at] = total_r
            tot[(i,) + at_i] = total_i
        return c

    lax.fori_loop(0, (chans // 8) * lane_tiles, products, 0, unroll=True)
    result = jnp.dot(
        tot[...].reshape(count, 2 * block).astype(BF16), tab_i[...], preferred_element_type=F32
    ).astype(BF16)
    for j in range(blocks):
        at = (j % per_long) * block_len
        r0 = (j // per_long) * chans
        yn[j] = result[r0 : r0 + chans, at : at + block_len]
    def back_copy(peer):
        return pltpu.make_async_remote_copy(
            src_ref=ys.at[pl.ds(peer * held, held)], dst_ref=yr.at[:, mine, :],
            send_sem=ex_send.at[2], recv_sem=ex_recv.at[2],
            device_id={"ctx": peer}, device_id_type=pl.DeviceIdType.MESH,
        )

    for d in near[::-1] + [0]:
        peer = (me + d) % nctx
        for b in range(held):
            ys[peer * held + b] = yn[ord_ref[peer * held + b]]
        if d > 0:
            back_copy(peer).start()
    own_back = pltpu.make_async_copy(
        ys.at[pl.ds(me * held, held)], yr.at[:, mine, :], own_sem.at[2]
    )
    own_back.start()
    wait_bytes(wo, w_sem.at[3])
    own_back.wait()

    wait_bytes(yr.at[:, pl.ds(0, width - chans), :], ex_recv.at[2])

    for b in range(held):
        for c in range(0, width, 128):
            value = p1t[b, c : c + 128, :].astype(F32) * yr[b, c : c + 128, :].astype(F32)
            gated[b * block_len : (b + 1) * block_len, c : c + 128] = value.T.astype(BF16)

    targets = {"a": over, "bz": over, "bu": up, "bd": dn, "d": over, "eu": up, "ed": dn}
    names = ("a", "bu", "bd", "c", "d", "eu", "ed", "bz")

    def place(name, c):
        return {("bz", 0): 4, ("bz", 3): 11}.get((name, c), names.index(name) * 4 + c)

    def rs_copy(name, c):
        m = place(name, c)
        target = targets[name] if name != "c" else up if c < 2 else dn
        return pltpu.make_async_remote_copy(
            src_ref=rout.at[m], dst_ref=rin.at[m], send_sem=rs_send.at[0], recv_sem=rs_recv.at[m],
            device_id=target, device_id_type=pl.DeviceIdType.MESH,
        )

    def send(name, c, value):
        rout[place(name, c)] = value.astype(BF16)
        rs_copy(name, c).start()

    def receive(name, c):
        rs_copy(name, c).wait_recv()
        return rin[place(name, c)].astype(F32)

    def out_part(slot, h):
        return jnp.dot(gated[...], wo[slot, :, h * half : (h + 1) * half], preferred_element_type=F32)

    def share(slot, c):
        return part[slot * 2 + c // 2, (c % 2) * quarter : (c % 2 + 1) * quarter, :]

    first, half_0, half_3 = out_part(7, 0), out_part(6, 0), out_part(5, 1)
    send("a", 0, first[:quarter])
    send("bu", 1, half_0[quarter:])
    send("bd", 2, half_3[:quarter])
    other = out_part(7, 1)
    send("a", 3, other[quarter:])
    send("a", 1, first[quarter:])
    send("a", 2, other[:quarter])
    for name, slot, h, order in (("bu", 6, 1, (0, 1)), ("bd", 5, 0, (1, 0))):
        value = out_part(slot, h)
        for r in order:
            send(name, h * 2 + r, value[r * quarter : (r + 1) * quarter])
    send("bz", 0, half_0[:quarter])
    send("bz", 3, half_3[quarter:])
    for slot in (4, 3, 2, 1, 0):
        for h in range(2):
            part[slot * 2 + h] = out_part(slot, h)
    send("c", 0, share(4, 0) + receive("a", 0))
    send("c", 3, share(4, 3) + receive("a", 3))
    send("ed", 1, share(1, 1))
    send("c", 1, share(4, 1) + receive("a", 1))
    send("eu", 2, share(2, 2))
    send("d", 1, share(3, 1) + receive("bu", 1) + receive("bd", 1))
    send("d", 2, share(3, 2) + receive("bu", 2) + receive("bd", 2))
    send("c", 2, share(4, 2) + receive("a", 2))
    send("ed", 0, share(1, 0))
    send("eu", 3, share(2, 3))
    send("d", 0, share(3, 0) + receive("bd", 0))
    send("d", 3, share(3, 3) + receive("bu", 3))
    send("eu", 0, share(2, 0) + receive("c", 0) + receive("bz", 0))
    send("ed", 3, share(1, 3) + receive("c", 3) + receive("bz", 3))
    send("eu", 1, share(2, 1) + receive("c", 1))
    send("ed", 2, share(1, 2) + receive("c", 2))
    for c in (0, 3, 1, 2):
        total = share(0, c) + receive("d", c)
        total = total + receive("eu", c) + receive("ed", c)
        at_r, at_c = (c % 2) * quarter, (c // 2) * half
        out_ref[at_r : at_r + quarter, at_c : at_c + half] = total.astype(BF16)

    wait_bytes(tok.at[pl.ds(2, 14)], ag_send.at[0])
    wait_bytes(taps_t.at[pl.ds(0, width - chans), :], ex_send.at[0])
    wait_bytes(mx.at[pl.ds(0, blocks - held)], ex_send.at[1])
    wait_bytes(mx.at[pl.ds(0, blocks - held)], ex_send.at[2])
    wait_bytes(rout, rs_send.at[0])


def local(nctx, nch, block, tokens, filter_taps, block_order, in_weights, out_weights):
    rows, width = tokens.shape
    blocks = block_order.shape[0]
    block_len = rows * nctx // blocks
    half = width // 2
    chans = width // nctx
    held = rows // block_len
    long_blocks = rows * nctx // block
    forward, inverse = spectral_tables(block)
    dims = (nctx, nch, rows, width, block_len, block)
    hbm = pl.BlockSpec(memory_space=pl.ANY)
    dma = pltpu.SemaphoreType.DMA
    return pl.pallas_call(
        functools.partial(kernel, dims),
        out_shape=pltpu.VMEM((rows, width), BF16),
        in_specs=[hbm] * 7,
        out_specs=pl.BlockSpec(memory_space=pltpu.VMEM),
        scratch_shapes=[
            pltpu.VMEM((16, rows, half), BF16),
            pltpu.VMEM((8, 3, width, width), BF16),
            pltpu.VMEM((8, width, width), BF16),
            pltpu.VMEM((3, rows, width), F32),
            pltpu.VMEM(forward.shape, BF16),
            pltpu.VMEM(inverse.shape, BF16),
            pltpu.VMEM((rows, width), BF16),
            pltpu.VMEM((width, rows), BF16),
            pltpu.VMEM((long_blocks, chans, block), BF16),
            pltpu.VMEM((long_blocks, chans, block), F32),
            pltpu.VMEM((long_blocks, chans, block), F32),
            pltpu.VMEM((long_blocks, chans, block), F32),
            pltpu.VMEM((held, width, block_len), BF16),
            pltpu.VMEM((blocks, chans, block_len), BF16),
            pltpu.VMEM((long_blocks, chans, block), BF16),
            pltpu.VMEM((long_blocks, chans, 2 * block), F32),
            pltpu.VMEM((long_blocks, chans, 2 * block), F32),
            pltpu.VMEM((blocks, chans, block_len), BF16),
            pltpu.VMEM((blocks, chans, block_len), BF16),
            pltpu.VMEM((held, width, block_len), BF16),
            pltpu.VMEM((held, width, block_len), BF16),
            pltpu.VMEM((rows, width), BF16),
            pltpu.VMEM((10, rows, half), F32),
            pltpu.VMEM((28, rows // 2, half), BF16),
            pltpu.VMEM((28, rows // 2, half), BF16),
            pltpu.SMEM((blocks,), jnp.int32),
            pltpu.SMEM((blocks,), jnp.int32),
            dma((5,)), dma((4,)),
            dma((1,)), dma((28,)),
            dma((3,)), dma((3,)),
            dma((1,)), dma((28,)),
            dma((3,)),
        ],
        compiler_params=pltpu.CompilerParams(
            collective_id=0, has_side_effects=True, vmem_limit_bytes=56 * 2**20
        ),
        name="hyena_layer",
    )(block_order, tokens, filter_taps, in_weights, out_weights, jnp.asarray(forward), jnp.asarray(inverse))


def solution(mesh):
    placed = (P("ctx", "ch"), P("ctx", "ch"), P(), P(None, None, "ch"), P("ch", None))
    body = functools.partial(local, mesh.shape["ctx"], mesh.shape["ch"], 512)
    return jax.shard_map(body, mesh=mesh, in_specs=placed, out_specs=P("ctx", "ch"), check_vma=False)
```

```python
import functools
import math

import jax
import jax.numpy as jnp
import ml_dtypes
import numpy as np
from jax import lax
from jax.experimental import pallas as pl
from jax.experimental.pallas import tpu as pltpu
from jax.sharding import PartitionSpec as P

F32 = jnp.float32
BF16 = jnp.bfloat16


def spectral_tables(block):
    length = 2 * block
    index = np.arange(block)
    angles = 2.0 * math.pi * ((index[:, None] * index[None, :]) % length) / length
    real, imag = np.cos(angles), -np.sin(angles)
    imag[:, 0] = 1.0 - 2.0 * (index % 2)
    forward = np.concatenate([real, imag], 1).astype(ml_dtypes.bfloat16)
    later = index + block
    back = 2.0 * math.pi * ((index[:, None] * later[None, :]) % length) / length
    real, imag = 2.0 * np.cos(back) / length, -2.0 * np.sin(back) / length
    real[0] = 1.0 / length
    imag[0] = (1.0 - 2.0 * (later % 2)) / length
    inverse = np.concatenate([real, imag], 0).astype(ml_dtypes.bfloat16)
    return forward, inverse


ARRIVALS = (
    (1, 0), (2, 3), (1, 1), (2, 2), (3, 1), "p10", (3, 2), "p21", (1, 2), (2, 1), (3, 0), "p30", (1, 3), (2, 0),
    (3, 3), "p11", "p20", "p31", (4, 0), (4, 3), (4, 1), (4, 2), "p40", "p41", "invert",
    (5, 0), (5, 1), "p50", (6, 3), (6, 2), "p61", (5, 2), (5, 3), "p51", (6, 1), (6, 0), "p60",
    (7, 0), (7, 1), "p70", (7, 2), (7, 3), "p71",
)
FORWARDS = {
    (1, 0): ((4, 0), (5, 0)), (1, 1): ((4, 1),), (2, 3): ((4, 3),), (2, 2): ((4, 2),),
    (3, 0): ((6, 0),), (3, 1): ((5, 1), (6, 1)), (3, 2): ((5, 2), (6, 2)), (3, 3): ((5, 3), (6, 3)),
    (4, 0): ((7, 0),), (4, 1): ((7, 1),), (4, 2): ((7, 2),), (4, 3): ((7, 3),),
}


def kernel(
    dims, order_ref, tokens_ref, taps_ref, w_in_ref, w_out_ref, tab_f_ref, tab_i_ref, out_ref,
    tok, wv, wo, acc, tab_f, tab_i, taps_v, taps_t, ft, fr, fi, fz, mt, mx, xn, sp, tot, yn, ys, yr,
    p1t, gated, part, rin, rout, ord_ref, inv_ref,
    load_sem, w_sem, ag_send, ag_recv, ex_send, ex_recv, rs_send, rs_recv, own_sem,
):
    nctx, nch, rows, width, block_len, block = dims
    half = width // 2
    ny = nch // 2
    chans = width // nctx
    blocks = nctx * rows // block_len
    held = rows // block_len
    long_blocks = nctx * rows // block
    per_long = block // block_len
    near = sorted(range(1, nctx), key=lambda d: min(d, nctx - d))
    me = lax.axis_index("ctx")
    ch = lax.axis_index("ch")
    z = ch // ny
    y = ch % ny
    zo = 1 - z
    y_up = (y + 1) % ny
    y_dn = (y + ny - 1) % ny
    y_far = (y + 2) % ny
    up = {"ch": z * ny + y_up}
    dn = {"ch": z * ny + y_dn}
    over = {"ch": zo * ny + y}
    shard_of = (
        z * ny + y, z * ny + y_dn, z * ny + y_up, zo * ny + y,
        z * ny + y_far, zo * ny + y_dn, zo * ny + y_up, zo * ny + y_far,
    )

    def wait_bytes(ref, sem):
        pltpu.make_async_copy(ref, ref, sem).wait()

    barrier = pltpu.get_barrier_semaphore()
    for neighbour in (up, dn, over):
        pl.semaphore_signal(barrier, inc=1, device_id=neighbour, device_id_type=pl.DeviceIdType.MESH)
    for d in near[::-1]:
        pl.semaphore_signal(
            barrier, inc=1, device_id={"ctx": (me + d) % nctx}, device_id_type=pl.DeviceIdType.MESH
        )
    pl.semaphore_wait(barrier, 3 + nctx - 1)

    quarter = rows // 2

    def chunk(slot, c):
        return tok.at[slot * 2 + c // 2, pl.ds((c % 2) * quarter, quarter)]

    def message(slot, c, source, target):
        if source is None:
            source = tokens_ref.at[pl.ds((c % 2) * quarter, quarter), pl.ds((c // 2) * half, half)]
        else:
            source = chunk(source, c)
        return pltpu.make_async_remote_copy(
            src_ref=source, dst_ref=chunk(slot, c), send_sem=ag_send.at[0],
            recv_sem=ag_recv.at[(slot - 1) * 4 + c], device_id=target,
            device_id_type=pl.DeviceIdType.MESH,
        )

    gather = {}
    for c in range(4):
        gather[1, c] = message(1, c, None, up)
        gather[2, c] = message(2, c, None, dn)
        gather[3, c] = message(3, c, None, over)
        gather[4, c] = message(4, c, 1, up) if c < 2 else message(4, c, 2, dn)
        gather[5, c] = message(5, c, 1, over) if c == 0 else message(5, c, 3, up)
        gather[6, c] = message(6, c, 3, dn)
        gather[7, c] = message(7, c, 4, over)
    for keys in zip(((1, 0), (1, 1), (1, 2), (1, 3)), ((2, 3), (2, 2), (2, 1), (2, 0)), ((3, 1), (3, 2), (3, 0), (3, 3))):
        for key in keys:
            gather[key].start()

    taps_load = pltpu.make_async_copy(taps_ref, taps_v, load_sem.at[0])
    tab_f_load = pltpu.make_async_copy(tab_f_ref, tab_f, load_sem.at[1])
    tab_i_load = pltpu.make_async_copy(tab_i_ref, tab_i, load_sem.at[2])
    order_load = pltpu.make_async_copy(order_ref, ord_ref, load_sem.at[3])
    w_group = (0, 1, 1, 1, 2, 2, 2, 2)
    taps_load.start()
    for h in range(2):
        pltpu.make_async_copy(tokens_ref.at[:, pl.ds(h * half, half)], tok.at[h], load_sem.at[4]).start()
    for slot in range(8):
        start = pl.multiple_of(shard_of[slot] * width, width)
        pltpu.make_async_copy(
            w_in_ref.at[:, pl.ds(start, width), :], wv.at[slot], w_sem.at[w_group[slot]]
        ).start()
        if slot == 3:
            tab_f_load.start()
            order_load.start()
    tab_i_load.start()
    for slot in range(8):
        start = pl.multiple_of(shard_of[slot] * width, width)
        pltpu.make_async_copy(
            w_out_ref.at[:, pl.ds(start, width)], wo.at[slot], w_sem.at[3]
        ).start()

    taps_load.wait()
    for r in range(0, rows, 128):
        for c in range(0, width, 128):
            piece = taps_v[r : r + 128, c : c + 128].astype(F32)
            taps_t[c : c + 128, r : r + 128] = piece.T.astype(BF16)

    per_rows = block // rows
    mine = pl.ds(pl.multiple_of(me * chans, chans), chans)
    my_lags = pl.ds(pl.multiple_of((me % per_rows) * rows, rows), rows)

    def channels_of(peer):
        return pl.ds(pl.multiple_of(peer * chans, chans), chans)

    def taps_copy(d):
        peer = (me + d) % nctx
        return pltpu.make_async_remote_copy(
            src_ref=taps_t.at[channels_of(peer), :], dst_ref=ft.at[me // per_rows, :, my_lags],
            send_sem=ex_send.at[0], recv_sem=ex_recv.at[0],
            device_id={"ctx": peer}, device_id_type=pl.DeviceIdType.MESH,
        )

    def start_taps(d, c):
        taps_copy(d).start()
        return c

    lax.fori_loop(1, nctx, start_taps, 0)
    own_taps = pltpu.make_async_copy(
        taps_t.at[mine, :], ft.at[me // per_rows, :, my_lags], own_sem.at[0]
    )
    own_taps.start()

    def invert(j, c):
        found = jnp.int32(0)
        for s in range(blocks):
            found = jnp.where(ord_ref[s] == j, jnp.int32(s), found)
        inv_ref[j] = found
        return c

    def project(slot, h, streams, first=False):
        left = tok[slot * 2 + h]
        for k in streams:
            value = jnp.dot(left, wv[slot, k, h * half : (h + 1) * half, :], preferred_element_type=F32)
            if first:
                acc[k] = value
            else:
                acc[k] += value

    def filter_spectra():
        own_taps.wait()
        wait_bytes(taps_t.at[pl.ds(0, width - chans), :], ex_recv.at[0])
        tab_f_load.wait()
        lane = lax.broadcasted_iota(jnp.int32, (chans, block), 1)
        sign = jnp.where(lane % 2 == 0, 1.0, -1.0).astype(F32)
        count = long_blocks * chans
        spectra = jnp.dot(ft[...].reshape(count, block), tab_f[...], preferred_element_type=F32)
        sp[...] = spectra.reshape(long_blocks, chans, 2 * block)
        before_r = jnp.zeros((chans, block), F32)
        before_i = jnp.zeros((chans, block), F32)
        for j in range(long_blocks):
            now_r, now_i = sp[j, :, :block], sp[j, :, block:]
            real = before_r + sign * now_r
            imag = before_i + sign * now_i
            fr[j] = real
            fi[j] = jnp.where(lane == 0, 0.0, imag)
            fz[j] = jnp.where(lane == 0, imag, real)
            before_r, before_i = now_r, now_i

    wait_bytes(tok.at[pl.ds(0, 2)], load_sem.at[4])
    wait_bytes(wv.at[pl.ds(0, 1)], w_sem.at[0])
    project(0, 0, (0, 1, 2), first=True)
    waited = 0
    for step in ("p01",) + ARRIVALS:
        if step == "invert":
            order_load.wait()
            lax.fori_loop(0, blocks, invert, 0)
        elif isinstance(step, str):
            slot, h = int(step[1]), int(step[2])
            if w_group[slot] > waited:
                waited = w_group[slot]
                wait_bytes(wv.at[pl.ds(1, 3)] if waited == 1 else wv.at[pl.ds(4, 4)], w_sem.at[waited])
            if step != ARRIVALS[-1]:
                project(slot, h, (0, 1, 2))
        else:
            gather[step].wait_recv()
            for key in FORWARDS.get(step, ()):
                gather[key].start()

    def mixed_copy(peer):
        return pltpu.make_async_remote_copy(
            src_ref=mt.at[:, channels_of(peer), :], dst_ref=mx.at[pl.ds(me * held, held)],
            send_sem=ex_send.at[1], recv_sem=ex_recv.at[1],
            device_id={"ctx": peer}, device_id_type=pl.DeviceIdType.MESH,
        )

    groups = width // 128
    members = nctx // groups
    wide = width // 2
    last = tok[15]
    far_half = ((me // members + groups // 2) % groups) // (groups // 2)
    for side in (far_half, 1 - far_half):
        c0 = pl.multiple_of(side * wide, 128)
        found = []
        for k in (0, 2):
            value = jnp.dot(last, wv[7, k, half:, pl.ds(c0, wide)], preferred_element_type=F32)
            found.append((acc[k, :, pl.ds(c0, wide)] + value).astype(BF16).astype(F32))
        mixed = found[0] * found[1]
        for g in range(groups // 2):
            for b in range(held):
                at = slice(b * block_len, (b + 1) * block_len)
                mt[b, pl.ds(pl.multiple_of(c0 + g * 128, 128), 128), :] = (
                    mixed[at, g * 128 : (g + 1) * 128].T.astype(BF16)
                )
            group = side * (groups // 2) + g
            for k in range(members):
                peer = group * members + (me + k) % members

                @pl.when(peer != me)
                def _():
                    mixed_copy(peer).start()
    own_mixed = pltpu.make_async_copy(
        mt.at[:, mine, :], mx.at[pl.ds(me * held, held)], own_sem.at[1]
    )
    own_mixed.start()

    project(7, 1, (1,))
    for c in range(0, width, 128):
        for b in range(held):
            at = slice(b * block_len, (b + 1) * block_len)
            p1t[b, c : c + 128, :] = acc[1, at, c : c + 128].T.astype(BF16)
    filter_spectra()
    tab_i_load.wait()

    own_mixed.wait()

    wait_bytes(mx.at[pl.ds(0, blocks - held)], ex_recv.at[1])

    for j in range(blocks):
        at = (j % per_long) * block_len
        xn[j // per_long, :, at : at + block_len] = mx[inv_ref[j]]
    count = long_blocks * chans
    spectra = jnp.dot(xn[...].reshape(count, block), tab_f[...], preferred_element_type=F32)
    sp[...] = spectra.reshape(long_blocks, chans, 2 * block)

    lane_tiles = block // 128

    def products(tile, c):
        r0 = pl.multiple_of((tile // lane_tiles) * 8, 8)
        f0 = pl.multiple_of((tile % lane_tiles) * 128, 128)
        at = (pl.ds(r0, 8), pl.ds(f0, 128))
        at_i = (pl.ds(r0, 8), pl.ds(block + f0, 128))
        data_r = [sp[(j,) + at] for j in range(long_blocks)]
        data_i = [sp[(j,) + at_i] for j in range(long_blocks)]
        filt_r = [fr[(j,) + at] for j in range(long_blocks)]
        filt_i = [fi[(j,) + at] for j in range(long_blocks)]
        filt_z = [fz[(j,) + at] for j in range(long_blocks)]
        for i in range(long_blocks):
            total_r = data_r[0] * filt_r[i] - data_i[0] * filt_i[i]
            total_i = data_r[0] * filt_i[i] + data_i[0] * filt_z[i]
            for j in range(1, i + 1):
                total_r = total_r + (data_r[j] * filt_r[i - j] - data_i[j] * filt_i[i - j])
                total_i = total_i + (data_r[j] * filt_i[i - j] + data_i[j] * filt_z[i - j])
            tot[(i,) + at] = total_r
            tot[(i,) + at_i] = total_i
        return c

    lax.fori_loop(0, (chans // 8) * lane_tiles, products, 0, unroll=True)
    result = jnp.dot(
        tot[...].reshape(count, 2 * block).astype(BF16), tab_i[...], preferred_element_type=F32
    ).astype(BF16)
    for j in range(blocks):
        at = (j % per_long) * block_len
        r0 = (j // per_long) * chans
        yn[j] = result[r0 : r0 + chans, at : at + block_len]
    def back_copy(peer):
        return pltpu.make_async_remote_copy(
            src_ref=ys.at[pl.ds(peer * held, held)], dst_ref=yr.at[:, mine, :],
            send_sem=ex_send.at[2], recv_sem=ex_recv.at[2],
            device_id={"ctx": peer}, device_id_type=pl.DeviceIdType.MESH,
        )

    for d in near[::-1] + [0]:
        peer = (me + d) % nctx
        for b in range(held):
            ys[peer * held + b] = yn[ord_ref[peer * held + b]]
        if d > 0:
            back_copy(peer).start()
    own_back = pltpu.make_async_copy(
        ys.at[pl.ds(me * held, held)], yr.at[:, mine, :], own_sem.at[2]
    )
    own_back.start()
    wait_bytes(wo, w_sem.at[3])
    own_back.wait()

    wait_bytes(yr.at[:, pl.ds(0, width - chans), :], ex_recv.at[2])

    for b in range(held):
        for c in range(0, width, 128):
            value = p1t[b, c : c + 128, :].astype(F32) * yr[b, c : c + 128, :].astype(F32)
            gated[b * block_len : (b + 1) * block_len, c : c + 128] = value.T.astype(BF16)

    targets = {"a": over, "bz": over, "bu": up, "bd": dn, "d": over, "eu": up, "ed": dn}
    names = ("a", "bu", "bd", "c", "d", "eu", "ed", "bz")

    def place(name, c):
        return {("bz", 0): 4, ("bz", 3): 11}.get((name, c), names.index(name) * 4 + c)

    def rs_copy(name, c):
        m = place(name, c)
        target = targets[name] if name != "c" else up if c < 2 else dn
        return pltpu.make_async_remote_copy(
            src_ref=rout.at[m], dst_ref=rin.at[m], send_sem=rs_send.at[0],
            recv_sem=rs_recv.at[m if m < 16 else 16 + c],
            device_id=target, device_id_type=pl.DeviceIdType.MESH,
        )

    def send(name, c, value):
        rout[place(name, c)] = value.astype(BF16)
        rs_copy(name, c).start()

    def receive(name, c):
        rs_copy(name, c).wait_recv()
        return rin[place(name, c)].astype(F32)

    def out_part(slot, h):
        return jnp.dot(gated[...], wo[slot, :, h * half : (h + 1) * half], preferred_element_type=F32)

    def share(slot, c):
        return part[slot * 2 + c // 2, (c % 2) * quarter : (c % 2 + 1) * quarter, :]

    first, half_0, half_3 = out_part(7, 0), out_part(6, 0), out_part(5, 1)
    send("a", 0, first[:quarter])
    send("bu", 1, half_0[quarter:])
    send("bd", 2, half_3[:quarter])
    other = out_part(7, 1)
    send("a", 3, other[quarter:])
    send("a", 1, first[quarter:])
    send("a", 2, other[:quarter])
    for name, slot, h, order in (("bu", 6, 1, (0, 1)), ("bd", 5, 0, (1, 0))):
        value = out_part(slot, h)
        for r in order:
            send(name, h * 2 + r, value[r * quarter : (r + 1) * quarter])
    send("bz", 0, half_0[:quarter])
    send("bz", 3, half_3[quarter:])
    for slot in (4, 3, 2, 1, 0):
        for h in range(2):
            part[slot * 2 + h] = out_part(slot, h)
    send("c", 0, share(4, 0) + receive("a", 0))
    send("c", 3, share(4, 3) + receive("a", 3))
    send("ed", 1, share(1, 1))
    send("c", 1, share(4, 1) + receive("a", 1))
    send("eu", 2, share(2, 2))
    send("d", 1, share(3, 1) + receive("bu", 1) + receive("bd", 1))
    send("d", 2, share(3, 2) + receive("bu", 2) + receive("bd", 2))
    send("c", 2, share(4, 2) + receive("a", 2))
    send("ed", 0, share(1, 0))
    send("eu", 3, share(2, 3))
    send("d", 0, share(3, 0) + receive("bd", 0))
    send("d", 3, share(3, 3) + receive("bu", 3))
    send("eu", 0, share(2, 0) + receive("c", 0) + receive("bz", 0))
    send("ed", 3, share(1, 3) + receive("c", 3) + receive("bz", 3))
    send("eu", 1, share(2, 1) + receive("c", 1))
    send("ed", 2, share(1, 2) + receive("c", 2))
    for c in (0, 3, 1, 2):
        wait_bytes(rin.at[pl.ds(0, 3)], rs_recv.at[16 + c])
        total = share(0, c)
        for name in ("d", "eu", "ed"):
            total = total + rin[place(name, c)].astype(F32)
        at_r, at_c = (c % 2) * quarter, (c // 2) * half
        out_ref[at_r : at_r + quarter, at_c : at_c + half] = total.astype(BF16)

    wait_bytes(tok.at[pl.ds(2, 14)], ag_send.at[0])
    wait_bytes(taps_t.at[pl.ds(0, width - chans), :], ex_send.at[0])
    wait_bytes(mx.at[pl.ds(0, blocks - held)], ex_send.at[1])
    wait_bytes(mx.at[pl.ds(0, blocks - held)], ex_send.at[2])
    wait_bytes(rout, rs_send.at[0])


def local(nctx, nch, block, tokens, filter_taps, block_order, in_weights, out_weights):
    rows, width = tokens.shape
    blocks = block_order.shape[0]
    block_len = rows * nctx // blocks
    half = width // 2
    chans = width // nctx
    held = rows // block_len
    long_blocks = rows * nctx // block
    forward, inverse = spectral_tables(block)
    dims = (nctx, nch, rows, width, block_len, block)
    hbm = pl.BlockSpec(memory_space=pl.ANY)
    dma = pltpu.SemaphoreType.DMA
    return pl.pallas_call(
        functools.partial(kernel, dims),
        out_shape=pltpu.VMEM((rows, width), BF16),
        in_specs=[hbm] * 7,
        out_specs=pl.BlockSpec(memory_space=pltpu.VMEM),
        scratch_shapes=[
            pltpu.VMEM((16, rows, half), BF16),
            pltpu.VMEM((8, 3, width, width), BF16),
            pltpu.VMEM((8, width, width), BF16),
            pltpu.VMEM((3, rows, width), F32),
            pltpu.VMEM(forward.shape, BF16),
            pltpu.VMEM(inverse.shape, BF16),
            pltpu.VMEM((rows, width), BF16),
            pltpu.VMEM((width, rows), BF16),
            pltpu.VMEM((long_blocks, chans, block), BF16),
            pltpu.VMEM((long_blocks, chans, block), F32),
            pltpu.VMEM((long_blocks, chans, block), F32),
            pltpu.VMEM((long_blocks, chans, block), F32),
            pltpu.VMEM((held, width, block_len), BF16),
            pltpu.VMEM((blocks, chans, block_len), BF16),
            pltpu.VMEM((long_blocks, chans, block), BF16),
            pltpu.VMEM((long_blocks, chans, 2 * block), F32),
            pltpu.VMEM((long_blocks, chans, 2 * block), F32),
            pltpu.VMEM((blocks, chans, block_len), BF16),
            pltpu.VMEM((blocks, chans, block_len), BF16),
            pltpu.VMEM((held, width, block_len), BF16),
            pltpu.VMEM((held, width, block_len), BF16),
            pltpu.VMEM((rows, width), BF16),
            pltpu.VMEM((10, rows, half), F32),
            pltpu.VMEM((28, rows // 2, half), BF16),
            pltpu.VMEM((28, rows // 2, half), BF16),
            pltpu.SMEM((blocks,), jnp.int32),
            pltpu.SMEM((blocks,), jnp.int32),
            dma((5,)), dma((4,)),
            dma((1,)), dma((28,)),
            dma((3,)), dma((3,)),
            dma((1,)), dma((20,)),
            dma((3,)),
        ],
        compiler_params=pltpu.CompilerParams(
            collective_id=0, has_side_effects=True, vmem_limit_bytes=56 * 2**20
        ),
        name="hyena_layer",
    )(block_order, tokens, filter_taps, in_weights, out_weights, jnp.asarray(forward), jnp.asarray(inverse))


def solution(mesh):
    placed = (P("ctx", "ch"), P("ctx", "ch"), P(), P(None, None, "ch"), P("ch", None))
    body = functools.partial(local, mesh.shape["ctx"], mesh.shape["ch"], 512)
    return jax.shard_map(body, mesh=mesh, in_specs=placed, out_specs=P("ctx", "ch"), check_vma=False)
```

```python
import functools
import math

import jax
import jax.numpy as jnp
import ml_dtypes
import numpy as np
from jax import lax
from jax.experimental import pallas as pl
from jax.experimental.pallas import tpu as pltpu
from jax.sharding import PartitionSpec as P

F32 = jnp.float32
BF16 = jnp.bfloat16


def spectral_tables(block):
    length = 2 * block
    index = np.arange(block)
    angles = 2.0 * math.pi * ((index[:, None] * index[None, :]) % length) / length
    real, imag = np.cos(angles), -np.sin(angles)
    imag[:, 0] = 1.0 - 2.0 * (index % 2)
    forward = np.concatenate([real, imag], 1).astype(ml_dtypes.bfloat16)
    later = index + block
    back = 2.0 * math.pi * ((index[:, None] * later[None, :]) % length) / length
    real, imag = 2.0 * np.cos(back) / length, -2.0 * np.sin(back) / length
    real[0] = 1.0 / length
    imag[0] = (1.0 - 2.0 * (later % 2)) / length
    inverse = np.concatenate([real, imag], 0).astype(ml_dtypes.bfloat16)
    return forward, inverse


ARRIVALS = (
    (1, 0), (2, 3), (1, 1), (2, 2), (3, 1), "p10", (3, 2), "p21", (1, 2), (2, 1), (3, 0), "p30", (1, 3), (2, 0),
    (3, 3), "p11", "p20", "p31", (4, 0), (4, 3), (4, 1), (4, 2), "p40", "p41", "invert",
    (5, 0), (5, 1), "p50", (6, 3), (6, 2), "p61", (5, 2), (5, 3), "p51", (6, 1), (6, 0), "p60",
    (7, 0), (7, 1), "p70", (7, 2), (7, 3), "p71",
)
FORWARDS = {
    (1, 0): ((4, 0), (5, 0)), (1, 1): ((4, 1),), (2, 3): ((4, 3),), (2, 2): ((4, 2),),
    (3, 0): ((6, 0),), (3, 1): ((5, 1), (6, 1)), (3, 2): ((5, 2), (6, 2)), (3, 3): ((5, 3), (6, 3)),
    (4, 0): ((7, 0),), (4, 1): ((7, 1),), (4, 2): ((7, 2),), (4, 3): ((7, 3),),
}


def kernel(
    dims, order_ref, tokens_ref, taps_ref, w_in_ref, w_out_ref, tab_f_ref, tab_i_ref, out_ref,
    tok, wv, wo, acc, tab_f, tab_i, taps_v, taps_t, ft, fr, fi, fz, mt, mx, xn, sp, tot, yn, ys, yr,
    p1t, gated, part, rin, rout, ord_ref, inv_ref,
    load_sem, w_sem, ag_send, ag_recv, ex_send, ex_recv, rs_send, rs_recv, own_sem,
):
    nctx, nch, rows, width, block_len, block = dims
    half = width // 2
    ny = nch // 2
    chans = width // nctx
    blocks = nctx * rows // block_len
    held = rows // block_len
    long_blocks = nctx * rows // block
    per_long = block // block_len
    near = sorted(range(1, nctx), key=lambda d: min(d, nctx - d))
    me = lax.axis_index("ctx")
    ch = lax.axis_index("ch")
    z = ch // ny
    y = ch % ny
    zo = 1 - z
    y_up = (y + 1) % ny
    y_dn = (y + ny - 1) % ny
    y_far = (y + 2) % ny
    up = {"ch": z * ny + y_up}
    dn = {"ch": z * ny + y_dn}
    over = {"ch": zo * ny + y}
    shard_of = (
        z * ny + y, z * ny + y_dn, z * ny + y_up, zo * ny + y,
        z * ny + y_far, zo * ny + y_dn, zo * ny + y_up, zo * ny + y_far,
    )

    def wait_bytes(ref, sem):
        pltpu.make_async_copy(ref, ref, sem).wait()

    barrier = pltpu.get_barrier_semaphore()
    for neighbour in (up, dn, over):
        pl.semaphore_signal(barrier, inc=1, device_id=neighbour, device_id_type=pl.DeviceIdType.MESH)
    for d in near[::-1]:
        pl.semaphore_signal(
            barrier, inc=1, device_id={"ctx": (me + d) % nctx}, device_id_type=pl.DeviceIdType.MESH
        )
    pl.semaphore_wait(barrier, 3 + nctx - 1)

    quarter = rows // 2

    def chunk(slot, c):
        return tok.at[slot * 2 + c // 2, pl.ds((c % 2) * quarter, quarter)]

    def message(slot, c, source, target):
        if source is None:
            source = tokens_ref.at[pl.ds((c % 2) * quarter, quarter), pl.ds((c // 2) * half, half)]
        else:
            source = chunk(source, c)
        return pltpu.make_async_remote_copy(
            src_ref=source, dst_ref=chunk(slot, c), send_sem=ag_send.at[0],
            recv_sem=ag_recv.at[(slot - 1) * 4 + c], device_id=target,
            device_id_type=pl.DeviceIdType.MESH,
        )

    gather = {}
    for c in range(4):
        gather[1, c] = message(1, c, None, up)
        gather[2, c] = message(2, c, None, dn)
        gather[3, c] = message(3, c, None, over)
        gather[4, c] = message(4, c, 1, up) if c < 2 else message(4, c, 2, dn)
        gather[5, c] = message(5, c, 1, over) if c == 0 else message(5, c, 3, up)
        gather[6, c] = message(6, c, 3, dn)
        gather[7, c] = message(7, c, 4, over)
    for keys in zip(((3, 1), (3, 2), (3, 0), (3, 3)), ((1, 0), (1, 1), (1, 2), (1, 3)), ((2, 3), (2, 2), (2, 1), (2, 0))):
        for key in keys:
            gather[key].start()

    taps_load = pltpu.make_async_copy(taps_ref, taps_v, load_sem.at[0])
    tab_f_load = pltpu.make_async_copy(tab_f_ref, tab_f, load_sem.at[1])
    tab_i_load = pltpu.make_async_copy(tab_i_ref, tab_i, load_sem.at[2])
    order_load = pltpu.make_async_copy(order_ref, ord_ref, load_sem.at[3])
    w_group = (0, 1, 1, 1, 2, 2, 2, 2)
    taps_load.start()
    for h in range(2):
        pltpu.make_async_copy(tokens_ref.at[:, pl.ds(h * half, half)], tok.at[h], load_sem.at[4]).start()
    for slot in range(8):
        start = pl.multiple_of(shard_of[slot] * width, width)
        pltpu.make_async_copy(
            w_in_ref.at[:, pl.ds(start, width), :], wv.at[slot], w_sem.at[w_group[slot]]
        ).start()
        if slot == 3:
            tab_f_load.start()
            order_load.start()
    tab_i_load.start()
    for slot in range(8):
        start = pl.multiple_of(shard_of[slot] * width, width)
        pltpu.make_async_copy(
            w_out_ref.at[:, pl.ds(start, width)], wo.at[slot], w_sem.at[3]
        ).start()

    taps_load.wait()
    for r in range(0, rows, 128):
        for c in range(0, width, 128):
            piece = taps_v[r : r + 128, c : c + 128].astype(F32)
            taps_t[c : c + 128, r : r + 128] = piece.T.astype(BF16)

    per_rows = block // rows
    mine = pl.ds(pl.multiple_of(me * chans, chans), chans)
    my_lags = pl.ds(pl.multiple_of((me % per_rows) * rows, rows), rows)

    def channels_of(peer):
        return pl.ds(pl.multiple_of(peer * chans, chans), chans)

    def taps_copy(d):
        peer = (me + d) % nctx
        return pltpu.make_async_remote_copy(
            src_ref=taps_t.at[channels_of(peer), :], dst_ref=ft.at[me // per_rows, :, my_lags],
            send_sem=ex_send.at[0], recv_sem=ex_recv.at[0],
            device_id={"ctx": peer}, device_id_type=pl.DeviceIdType.MESH,
        )

    def start_taps(d, c):
        taps_copy(d).start()
        return c

    lax.fori_loop(1, nctx, start_taps, 0)
    own_taps = pltpu.make_async_copy(
        taps_t.at[mine, :], ft.at[me // per_rows, :, my_lags], own_sem.at[0]
    )
    own_taps.start()

    def invert(j, c):
        found = jnp.int32(0)
        for s in range(blocks):
            found = jnp.where(ord_ref[s] == j, jnp.int32(s), found)
        inv_ref[j] = found
        return c

    def project(slot, h, streams, first=False):
        left = tok[slot * 2 + h]
        for k in streams:
            value = jnp.dot(left, wv[slot, k, h * half : (h + 1) * half, :], preferred_element_type=F32)
            if first:
                acc[k] = value
            else:
                acc[k] += value

    def filter_spectra():
        own_taps.wait()
        wait_bytes(taps_t.at[pl.ds(0, width - chans), :], ex_recv.at[0])
        tab_f_load.wait()
        lane = lax.broadcasted_iota(jnp.int32, (chans, block), 1)
        sign = jnp.where(lane % 2 == 0, 1.0, -1.0).astype(F32)
        count = long_blocks * chans
        spectra = jnp.dot(ft[...].reshape(count, block), tab_f[...], preferred_element_type=F32)
        sp[...] = spectra.reshape(long_blocks, chans, 2 * block)
        before_r = jnp.zeros((chans, block), F32)
        before_i = jnp.zeros((chans, block), F32)
        for j in range(long_blocks):
            now_r, now_i = sp[j, :, :block], sp[j, :, block:]
            real = before_r + sign * now_r
            imag = before_i + sign * now_i
            fr[j] = real
            fi[j] = jnp.where(lane == 0, 0.0, imag)
            fz[j] = jnp.where(lane == 0, imag, real)
            before_r, before_i = now_r, now_i

    wait_bytes(tok.at[pl.ds(0, 2)], load_sem.at[4])
    wait_bytes(wv.at[pl.ds(0, 1)], w_sem.at[0])
    project(0, 0, (0, 1, 2), first=True)
    waited = 0
    for step in ("p01",) + ARRIVALS:
        if step == "invert":
            order_load.wait()
            lax.fori_loop(0, blocks, invert, 0)
        elif isinstance(step, str):
            slot, h = int(step[1]), int(step[2])
            if w_group[slot] > waited:
                waited = w_group[slot]
                wait_bytes(wv.at[pl.ds(1, 3)] if waited == 1 else wv.at[pl.ds(4, 4)], w_sem.at[waited])
            if step != ARRIVALS[-1]:
                project(slot, h, (0, 1, 2))
        else:
            gather[step].wait_recv()
            for key in FORWARDS.get(step, ()):
                gather[key].start()

    def mixed_copy(peer):
        return pltpu.make_async_remote_copy(
            src_ref=mt.at[:, channels_of(peer), :], dst_ref=mx.at[pl.ds(me * held, held)],
            send_sem=ex_send.at[1], recv_sem=ex_recv.at[1],
            device_id={"ctx": peer}, device_id_type=pl.DeviceIdType.MESH,
        )

    groups = width // 128
    members = nctx // groups
    wide = width // 2
    last = tok[15]
    far_half = ((me // members + groups // 2) % groups) // (groups // 2)
    for side in (far_half, 1 - far_half):
        c0 = pl.multiple_of(side * wide, 128)
        found = []
        for k in (0, 2):
            value = jnp.dot(last, wv[7, k, half:, pl.ds(c0, wide)], preferred_element_type=F32)
            found.append((acc[k, :, pl.ds(c0, wide)] + value).astype(BF16).astype(F32))
        mixed = found[0] * found[1]
        for g in range(groups // 2):
            for b in range(held):
                at = slice(b * block_len, (b + 1) * block_len)
                mt[b, pl.ds(pl.multiple_of(c0 + g * 128, 128), 128), :] = (
                    mixed[at, g * 128 : (g + 1) * 128].T.astype(BF16)
                )
            group = side * (groups // 2) + g
            for k in range(members):
                peer = group * members + (me + k) % members

                @pl.when(peer != me)
                def _():
                    mixed_copy(peer).start()
    own_mixed = pltpu.make_async_copy(
        mt.at[:, mine, :], mx.at[pl.ds(me * held, held)], own_sem.at[1]
    )
    own_mixed.start()

    project(7, 1, (1,))
    for c in range(0, width, 128):
        for b in range(held):
            at = slice(b * block_len, (b + 1) * block_len)
            p1t[b, c : c + 128, :] = acc[1, at, c : c + 128].T.astype(BF16)
    filter_spectra()
    tab_i_load.wait()

    own_mixed.wait()

    wait_bytes(mx.at[pl.ds(0, blocks - held)], ex_recv.at[1])

    for j in range(blocks):
        at = (j % per_long) * block_len
        xn[j // per_long, :, at : at + block_len] = mx[inv_ref[j]]
    count = long_blocks * chans
    spectra = jnp.dot(xn[...].reshape(count, block), tab_f[...], preferred_element_type=F32)
    sp[...] = spectra.reshape(long_blocks, chans, 2 * block)

    lane_tiles = block // 128

    def products(tile, c):
        r0 = pl.multiple_of((tile // lane_tiles) * 16, 16)
        f0 = pl.multiple_of((tile % lane_tiles) * 128, 128)
        at = (pl.ds(r0, 16), pl.ds(f0, 128))
        at_i = (pl.ds(r0, 16), pl.ds(block + f0, 128))
        data_r = [sp[(j,) + at] for j in range(long_blocks)]
        data_i = [sp[(j,) + at_i] for j in range(long_blocks)]
        filt_r = [fr[(j,) + at] for j in range(long_blocks)]
        filt_i = [fi[(j,) + at] for j in range(long_blocks)]
        filt_z = [fz[(j,) + at] for j in range(long_blocks)]
        for i in range(long_blocks):
            total_r = data_r[0] * filt_r[i] - data_i[0] * filt_i[i]
            total_i = data_r[0] * filt_i[i] + data_i[0] * filt_z[i]
            for j in range(1, i + 1):
                total_r = total_r + (data_r[j] * filt_r[i - j] - data_i[j] * filt_i[i - j])
                total_i = total_i + (data_r[j] * filt_i[i - j] + data_i[j] * filt_z[i - j])
            tot[(i,) + at] = total_r.astype(BF16)
            tot[(i,) + at_i] = total_i.astype(BF16)
        return c

    lax.fori_loop(0, (chans // 16) * lane_tiles, products, 0, unroll=True)
    result = jnp.dot(
        tot[...].reshape(count, 2 * block), tab_i[...], preferred_element_type=F32
    ).astype(BF16)
    for j in range(blocks):
        at = (j % per_long) * block_len
        r0 = (j // per_long) * chans
        yn[j] = result[r0 : r0 + chans, at : at + block_len]
    def back_copy(peer):
        return pltpu.make_async_remote_copy(
            src_ref=ys.at[pl.ds(peer * held, held)], dst_ref=yr.at[:, mine, :],
            send_sem=ex_send.at[2], recv_sem=ex_recv.at[2],
            device_id={"ctx": peer}, device_id_type=pl.DeviceIdType.MESH,
        )

    for d in near[::-1] + [0]:
        peer = (me + d) % nctx
        for b in range(held):
            ys[peer * held + b] = yn[ord_ref[peer * held + b]]
        if d > 0:
            back_copy(peer).start()
    own_back = pltpu.make_async_copy(
        ys.at[pl.ds(me * held, held)], yr.at[:, mine, :], own_sem.at[2]
    )
    own_back.start()
    wait_bytes(wo, w_sem.at[3])
    own_back.wait()

    wait_bytes(yr.at[:, pl.ds(0, width - chans), :], ex_recv.at[2])

    for b in range(held):
        for c in range(0, width, 128):
            value = p1t[b, c : c + 128, :].astype(F32) * yr[b, c : c + 128, :].astype(F32)
            gated[b * block_len : (b + 1) * block_len, c : c + 128] = value.T.astype(BF16)

    targets = {"a": over, "bz": over, "bu": up, "bd": dn, "d": over, "eu": up, "ed": dn}
    names = ("a", "bu", "bd", "c", "d", "eu", "ed", "bz")

    def place(name, c):
        return {("bz", 0): 4, ("bz", 3): 11}.get((name, c), names.index(name) * 4 + c)

    def rs_copy(name, c):
        m = place(name, c)
        target = targets[name] if name != "c" else up if c < 2 else dn
        return pltpu.make_async_remote_copy(
            src_ref=rout.at[m], dst_ref=rin.at[m], send_sem=rs_send.at[0],
            recv_sem=rs_recv.at[m if m < 16 else 16 + c],
            device_id=target, device_id_type=pl.DeviceIdType.MESH,
        )

    def send(name, c, value):
        rout[place(name, c)] = value.astype(BF16)
        rs_copy(name, c).start()

    def receive(name, c):
        rs_copy(name, c).wait_recv()
        return rin[place(name, c)].astype(F32)

    def out_part(slot, h):
        return jnp.dot(gated[...], wo[slot, :, h * half : (h + 1) * half], preferred_element_type=F32)

    def share(slot, c):
        return part[slot * 2 + c // 2, (c % 2) * quarter : (c % 2 + 1) * quarter, :]

    first, half_0, half_3 = out_part(7, 0), out_part(6, 0), out_part(5, 1)
    send("a", 0, first[:quarter])
    send("bu", 1, half_0[quarter:])
    send("bd", 2, half_3[:quarter])
    other = out_part(7, 1)
    send("a", 3, other[quarter:])
    send("a", 1, first[quarter:])
    send("a", 2, other[:quarter])
    for name, slot, h, order in (("bu", 6, 1, (0, 1)), ("bd", 5, 0, (1, 0))):
        value = out_part(slot, h)
        for r in order:
            send(name, h * 2 + r, value[r * quarter : (r + 1) * quarter])
    send("bz", 0, half_0[:quarter])
    send("bz", 3, half_3[quarter:])
    for slot in (4, 3, 2, 1, 0):
        for h in range(2):
            part[slot * 2 + h] = out_part(slot, h)
    send("c", 0, share(4, 0) + receive("a", 0))
    send("c", 3, share(4, 3) + receive("a", 3))
    send("ed", 1, share(1, 1))
    send("c", 1, share(4, 1) + receive("a", 1))
    send("eu", 2, share(2, 2))
    send("d", 1, share(3, 1) + receive("bu", 1) + receive("bd", 1))
    send("d", 2, share(3, 2) + receive("bu", 2) + receive("bd", 2))
    send("c", 2, share(4, 2) + receive("a", 2))
    send("ed", 0, share(1, 0))
    send("eu", 3, share(2, 3))
    send("d", 0, share(3, 0) + receive("bd", 0))
    send("d", 3, share(3, 3) + receive("bu", 3))
    send("eu", 0, share(2, 0) + receive("c", 0) + receive("bz", 0))
    send("ed", 3, share(1, 3) + receive("c", 3) + receive("bz", 3))
    send("eu", 1, share(2, 1) + receive("c", 1))
    send("ed", 2, share(1, 2) + receive("c", 2))
    for c in (0, 3, 1, 2):
        wait_bytes(rin.at[pl.ds(0, 3)], rs_recv.at[16 + c])
        total = share(0, c)
        for name in ("d", "eu", "ed"):
            total = total + rin[place(name, c)].astype(F32)
        at_r, at_c = (c % 2) * quarter, (c // 2) * half
        out_ref[at_r : at_r + quarter, at_c : at_c + half] = total.astype(BF16)

    wait_bytes(tok.at[pl.ds(2, 14)], ag_send.at[0])
    wait_bytes(taps_t.at[pl.ds(0, width - chans), :], ex_send.at[0])
    wait_bytes(mx.at[pl.ds(0, blocks - held)], ex_send.at[1])
    wait_bytes(mx.at[pl.ds(0, blocks - held)], ex_send.at[2])
    wait_bytes(rout, rs_send.at[0])


def local(nctx, nch, block, tokens, filter_taps, block_order, in_weights, out_weights):
    rows, width = tokens.shape
    blocks = block_order.shape[0]
    block_len = rows * nctx // blocks
    half = width // 2
    chans = width // nctx
    held = rows // block_len
    long_blocks = rows * nctx // block
    forward, inverse = spectral_tables(block)
    dims = (nctx, nch, rows, width, block_len, block)
    hbm = pl.BlockSpec(memory_space=pl.ANY)
    dma = pltpu.SemaphoreType.DMA
    return pl.pallas_call(
        functools.partial(kernel, dims),
        out_shape=pltpu.VMEM((rows, width), BF16),
        in_specs=[hbm] * 7,
        out_specs=pl.BlockSpec(memory_space=pltpu.VMEM),
        scratch_shapes=[
            pltpu.VMEM((16, rows, half), BF16),
            pltpu.VMEM((8, 3, width, width), BF16),
            pltpu.VMEM((8, width, width), BF16),
            pltpu.VMEM((3, rows, width), F32),
            pltpu.VMEM(forward.shape, BF16),
            pltpu.VMEM(inverse.shape, BF16),
            pltpu.VMEM((rows, width), BF16),
            pltpu.VMEM((width, rows), BF16),
            pltpu.VMEM((long_blocks, chans, block), BF16),
            pltpu.VMEM((long_blocks, chans, block), F32),
            pltpu.VMEM((long_blocks, chans, block), F32),
            pltpu.VMEM((long_blocks, chans, block), F32),
            pltpu.VMEM((held, width, block_len), BF16),
            pltpu.VMEM((blocks, chans, block_len), BF16),
            pltpu.VMEM((long_blocks, chans, block), BF16),
            pltpu.VMEM((long_blocks, chans, 2 * block), F32),
            pltpu.VMEM((long_blocks, chans, 2 * block), BF16),
            pltpu.VMEM((blocks, chans, block_len), BF16),
            pltpu.VMEM((blocks, chans, block_len), BF16),
            pltpu.VMEM((held, width, block_len), BF16),
            pltpu.VMEM((held, width, block_len), BF16),
            pltpu.VMEM((rows, width), BF16),
            pltpu.VMEM((10, rows, half), F32),
            pltpu.VMEM((28, rows // 2, half), BF16),
            pltpu.VMEM((28, rows // 2, half), BF16),
            pltpu.SMEM((blocks,), jnp.int32),
            pltpu.SMEM((blocks,), jnp.int32),
            dma((5,)), dma((4,)),
            dma((1,)), dma((28,)),
            dma((3,)), dma((3,)),
            dma((1,)), dma((20,)),
            dma((3,)),
        ],
        compiler_params=pltpu.CompilerParams(
            collective_id=0, has_side_effects=True, vmem_limit_bytes=56 * 2**20
        ),
        name="hyena_layer",
    )(block_order, tokens, filter_taps, in_weights, out_weights, jnp.asarray(forward), jnp.asarray(inverse))


def solution(mesh):
    placed = (P("ctx", "ch"), P("ctx", "ch"), P(), P(None, None, "ch"), P("ch", None))
    body = functools.partial(local, mesh.shape["ctx"], mesh.shape["ch"], 512)
    return jax.shard_map(body, mesh=mesh, in_specs=placed, out_specs=P("ctx", "ch"), check_vma=False)
```
